32 devices in a mesh: adapter: 8 (over z, core), tensor: 4 (over y, x).
Axes of the slice: x: 2, y: 2, z: 4, core: 2. Of those that a mesh axis runs over, the one named last changes fastest.
Arguments:
- attn_output: bfloat16 [2048, 8192], P('adapter', 'tensor'), may hold values from -6 to 6
- output_grad: bfloat16 [2048, 8192], P(('adapter', 'tensor')), may hold values from -6 to 6
- adapter_ids: int32 [2048], P('adapter'), may hold values from 0 to 255, as said below
- base_weight: bfloat16 [8192, 8192], P('tensor', 'adapter'), may hold values from -0.0625 to 0.0625
- adapter_down: bfloat16 [8192, 4096], P('tensor', 'adapter'), may hold values from -0.1796875 to 0.1796875
- adapter_up: bfloat16 [4096, 8192], P('adapter', 'tensor'), may hold values from -0.0625 to 0.0625
Outputs:
- attention_output_gradient: bfloat16 [2048, 8192], P('adapter', 'tensor')
- down_grad: float32 [8192, 4096], P('tensor', 'adapter')
- up_grad: float32 [4096, 8192], P('adapter', 'tensor')
The draws below stay inside these ranges and needn't reach their ends.
Inputs may be any that keep to these rules, and one draw needn't show every extreme that they name: `adapter_ids`: the 256 tokens of each index of adapter form one block; the owner of adapter a is a // 32. At most 80 tokens of a block have adapters of one owner, and one owner, drawn from the seed, gets exactly 80 tokens of every block.
All inputs are finite; a program needn't handle non-finite values.
Results may differ from the reference program's by a relative error of at most 0.007.
Values may be sent and summed in bfloat16 or wider, within the bound.
No kernel may reach another device: no remote copies, remote signals or barrier semaphores. Data moves between devices by JAX's collectives and lax.ppermute only.
A program may use at most 128 MiB of HBM per device.

```python
import jax
import jax.numpy as jnp
from jax import lax

MODEL_WIDTH = 8192
ADAPTER_RANK = 16
ADP_DEV = 32
TOK_DEV = 256
TOKEN_TOTAL = 2048
ADAPTERS = 256
CAP = 80
SLOTS = 640


def draw_adapter_ids(key, part):
    owners = ADAPTERS // ADP_DEV
    busy_key, row_key, local_key = jax.random.split(jax.random.fold_in(key, 17), 3)
    busiest = jax.random.randint(busy_key, (), 0, owners)

    def one_block(block_key):
        pick_key, order_key = jax.random.split(block_key)
        chosen = jax.random.permutation(pick_key, (owners - 1) * CAP)[:TOK_DEV - CAP]
        others = (chosen // CAP).astype(jnp.int32)
        others = others + (others >= busiest).astype(jnp.int32)
        all_rows = jnp.concatenate([jnp.full((CAP,), busiest, jnp.int32), others])
        return jax.random.permutation(order_key, all_rows)
    block_keys = jax.random.split(row_key, owners)
    owner_ids = jax.vmap(one_block)(block_keys).reshape(-1)
    local_ids = jax.random.randint(local_key, (TOKEN_TOTAL,), 0, ADP_DEV)
    return (owner_ids * ADP_DEV + local_ids).astype(jnp.int32)


def block_levels(stream_key, dims, shards, smallest, high):
    loudness, own = 1.0, jax.random.fold_in(stream_key, 6)
    for axis_at, parts in shards:
        draws = jnp.exp(jax.random.uniform(jax.random.fold_in(own, axis_at), (parts,), jnp.float32, smallest / len(shards), high / len(shards)))
        loudness = loudness * jnp.repeat(draws, dims[axis_at] // parts).reshape([-1 if axis == axis_at else 1 for axis in range(len(dims))])
    return loudness


def normal_values(stream_key, shape, scale, limit, cuts=(), kind=jnp.bfloat16):
    drawn = jax.random.normal(stream_key, shape, jnp.float32) * scale
    if len(cuts) > 0:
        drawn = block_levels(stream_key, shape, cuts, -0.22, 0.18) * drawn
    return jnp.clip(drawn, min=-limit, max=limit).astype(kind)


def setup_inputs(seed: int = 0) -> dict:
    keys = jax.random.split(jax.random.key(seed), 7)
    return {
        "attn_output": normal_values(keys[0], (TOKEN_TOTAL, MODEL_WIDTH), 1.0, 6.0, ((0, 8), (1, 4))),
        "output_grad": normal_values(keys[1], (TOKEN_TOTAL, MODEL_WIDTH), 1.0, 6.0, ((0, 32),)),
        "adapter_ids": draw_adapter_ids(jax.random.fold_in(keys[6], 71), 0),
        "base_weight": normal_values(keys[3], (MODEL_WIDTH, MODEL_WIDTH), MODEL_WIDTH ** -0.5, 0.0625, ((0, 4), (1, 8))),
        "adapter_down": normal_values(keys[4], (MODEL_WIDTH, ADAPTERS * ADAPTER_RANK), 0.03, 0.1796875, ((0, 4), (1, 8))),
        "adapter_up": normal_values(keys[5], (ADAPTERS * ADAPTER_RANK, MODEL_WIDTH), MODEL_WIDTH ** -0.5, 0.0625, ((0, 8), (1, 4))),
    }


ADAPTER_SCALE = 2.0


def reference(attn_output, output_grad, adapter_ids, base_weight, adapter_down, adapter_up):
    owners = ADAPTERS // ADP_DEV
    block_width = ADP_DEV * ADAPTER_RANK
    frozen_output = jnp.dot(output_grad, base_weight.T, preferred_element_type=jnp.float32)
    owner_of = (adapter_ids // ADP_DEV).astype(jnp.int32)
    local_of = (adapter_ids % ADP_DEV).astype(jnp.int32)
    sorted_token_order = jnp.argsort(owner_of, stable=True).astype(jnp.int32)
    sorted_owner = owner_of[sorted_token_order]
    sorted_local = local_of[sorted_token_order]
    sorted_inputs = attn_output[sorted_token_order]
    sorted_grads = output_grad[sorted_token_order]
    member = (owner_of[:, None] == jnp.arange(owners, dtype=jnp.int32)[None, :]).astype(jnp.int32)
    counts = jnp.sum(member, axis=0).astype(jnp.int32)
    offsets = (jnp.cumsum(counts) - counts).astype(jnp.int32)

    def one_owner(running_total, owner_index):
        leading_row = jnp.minimum(offsets[owner_index], TOKEN_TOTAL - SLOTS).astype(jnp.int32)
        rows_inputs = lax.dynamic_slice_in_dim(sorted_inputs, leading_row, SLOTS, 0)
        rows_grads = lax.dynamic_slice_in_dim(sorted_grads, leading_row, SLOTS, 0)
        rows_owner = lax.dynamic_slice_in_dim(sorted_owner, leading_row, SLOTS, 0)
        rows_local = lax.dynamic_slice_in_dim(sorted_local, leading_row, SLOTS, 0)
        down_weight_block = lax.dynamic_slice_in_dim(adapter_down, (owner_index * block_width).astype(jnp.int32), block_width, 1)
        up_block = lax.dynamic_slice_in_dim(adapter_up, (owner_index * block_width).astype(jnp.int32), block_width, 0)
        chosen = jnp.logical_and(rows_owner[:, None] == owner_index, rows_local[:, None] == jnp.arange(ADP_DEV, dtype=jnp.int32)[None, :]).astype(jnp.float32)
        spread = jnp.repeat(chosen, ADAPTER_RANK, axis=1)
        rank_inputs = (jnp.dot(rows_inputs, down_weight_block, preferred_element_type=jnp.float32) * spread).reshape(SLOTS, ADP_DEV, ADAPTER_RANK).sum(axis=1)
        rank_gradients = (jnp.dot(rows_grads, up_block.T, preferred_element_type=jnp.float32) * spread).reshape(SLOTS, ADP_DEV, ADAPTER_RANK).sum(axis=1)
        scaled_up_weight = (ADAPTER_SCALE * rank_inputs).astype(jnp.bfloat16)
        rank_gradient = (ADAPTER_SCALE * rank_gradients).astype(jnp.bfloat16)
        spread_half = spread.astype(jnp.bfloat16)
        wide_gradient = jnp.tile(rank_gradient, (1, ADP_DEV)) * spread_half
        up_wide = jnp.tile(scaled_up_weight, (1, ADP_DEV)) * spread_half
        down_part = jnp.dot(rows_inputs.T, wide_gradient, preferred_element_type=jnp.float32)
        up_part = jnp.dot(up_wide.T, rows_grads, preferred_element_type=jnp.float32)
        adapter_block = jnp.dot(wide_gradient, down_weight_block.T, preferred_element_type=jnp.float32).astype(jnp.bfloat16)
        adapter_block = lax.optimization_barrier(adapter_block).astype(jnp.float32)
        current_block = lax.dynamic_slice_in_dim(running_total, leading_row, SLOTS, 0)
        running_total = lax.dynamic_update_slice_in_dim(running_total, current_block + adapter_block, leading_row, 0)
        return running_total, (down_part, up_part)

    running_total, (down_parts, up_parts) = lax.scan(one_owner, jnp.zeros((TOKEN_TOTAL, MODEL_WIDTH), jnp.float32), jnp.arange(owners, dtype=jnp.int32))
    adapter_contribution = jnp.zeros((TOKEN_TOTAL, MODEL_WIDTH), jnp.float32).at[sorted_token_order].set(running_total)
    attention_output_gradient = (frozen_output + adapter_contribution).astype(jnp.bfloat16)
    down_grad = jnp.transpose(down_parts, (1, 0, 2)).reshape(MODEL_WIDTH, ADAPTERS * ADAPTER_RANK)
    up_grad = up_parts.reshape(ADAPTERS * ADAPTER_RANK, MODEL_WIDTH)
    return attention_output_gradient, down_grad, up_grad
```

```python
import jax
import jax.numpy as jnp
from jax import lax
from jax.sharding import PartitionSpec as P

ADAPTER_RANK = 16
ADAPTER_SCALE = 2.0
F32 = jnp.float32
BF16 = jnp.bfloat16


def per_device(attn, grad, ids, weight, down, up):
    owners = lax.axis_size("adapter")
    tensors = lax.axis_size("tensor")
    planes = owners // 2
    half_ring = planes // 2
    me = lax.axis_index("adapter")
    plane, core = me // 2, me % 2
    tensor = lax.axis_index("tensor")
    tokens, width = attn.shape
    sub = grad.shape[0]
    out_cols = weight.shape[1]
    rank_cols = down.shape[1]
    per_owner = rank_cols // ADAPTER_RANK

    up_pairs = [(2 * z + c, 2 * ((z + 1) % planes) + c) for z in range(planes) for c in range(2)]
    down_pairs = [(dst, src) for src, dst in up_pairs]
    core_pairs = [(a, a ^ 1) for a in range(owners)]

    def send_up(x):
        return lax.ppermute(x, "adapter", up_pairs)

    def send_down(x):
        return lax.ppermute(x, "adapter", down_pairs)

    def swap(x):
        return lax.ppermute(x, "adapter", core_pairs)

    def flip(x, bit):
        return lax.ppermute(x, "tensor", [(t, t ^ bit) for t in range(tensors)])

    bits = [1 << i for i in range(tensors.bit_length() - 1)]

    def after(x, *others):
        return lax.optimization_barrier((x, *others))[0]

    def plane_cols(offset, which):
        p = (plane + offset) % planes
        start = (2 * p + (core if which == 0 else 1 - core)) * out_cols
        return lax.dynamic_slice_in_dim(grad, start, out_cols, 1)

    going_up = [plane_cols(s, w) for s in range(1, half_ring) for w in range(2)] + [plane_cols(half_ring, 0)]
    going_down = [plane_cols(-s, w) for s in range(1, half_ring) for w in range(2)] + [plane_cols(half_ring, 1)]
    going_up = jnp.concatenate(going_up, axis=1)
    going_down = jnp.concatenate(going_down, axis=1)
    part = [None] * planes
    part[0] = jnp.concatenate([plane_cols(0, 0), plane_cols(0, 1)], axis=1)
    for s in range(1, half_ring + 1):
        going_up = send_up(going_up)
        going_down = send_down(going_down)
        if s < half_ring:
            part[s] = going_up[:, : 2 * out_cols]
            part[planes - s] = going_down[:, : 2 * out_cols]
            going_up = going_up[:, 2 * out_cols :]
            going_down = going_down[:, 2 * out_cols :]
        else:
            part[s] = jnp.concatenate([going_up, going_down], axis=1)

    grad_cols = lax.all_to_all(grad, "tensor", split_axis=1, concat_axis=0, tiled=True)
    other_weight = swap(weight)
    other_down = swap(down)
    all_ids = lax.all_gather(ids, "adapter", axis=0, tiled=False)

    stacked = jnp.stack(part, axis=0)
    first, second = stacked[:, : sub // 2], stacked[:, sub // 2 :]
    first, second = first[None], second[None]
    first_order, second_order = [0], [0]
    for low, high in zip(bits, reversed(bits)):
        first = jnp.concatenate([first, flip(first, low)], axis=0)
        first_order = first_order + [k ^ low for k in first_order]
        second = jnp.concatenate([second, flip(second, high)], axis=0)
        second_order = second_order + [k ^ high for k in second_order]

    def ring_gather(x, gate):
        if gate is not None:
            x = after(x, gate)
        blocks = [None] * planes
        blocks[0] = x
        above, below = x, x
        for s in range(1, half_ring):
            above, below = send_up(above), send_down(below)
            blocks[s], blocks[planes - s] = above, below
        above = send_up(above[: tokens // 2])
        below = send_down(below[tokens // 2 :])
        blocks[half_ring] = jnp.concatenate([above, below], axis=0)
        return blocks + [swap(b) for b in blocks]

    grad_blocks = ring_gather(grad_cols, part[half_ring])
    attn_blocks = ring_gather(attn, grad_blocks[half_ring])

    block_ids = [all_ids[2 * ((plane - d) % planes) + core] for d in range(planes)]
    block_ids += [all_ids[2 * ((plane - d) % planes) + 1 - core] for d in range(planes)]
    block_ids = jnp.concatenate(block_ids)
    own_mask = block_ids[None, :] == (me * per_owner + jnp.arange(per_owner, dtype=jnp.int32))[:, None]
    other_mask = block_ids[None, :] == ((me ^ 1) * per_owner + jnp.arange(per_owner, dtype=jnp.int32))[:, None]

    def ranks_of(projected):
        chosen = projected.reshape(per_owner, ADAPTER_RANK, -1)
        return jnp.sum(jnp.where(own_mask[:, None, :], chosen, 0.0), axis=0)

    def widen(ranks, mask):
        wide = jnp.where(mask[:, None, :], ranks[None], jnp.zeros((), BF16))
        return wide.reshape(rank_cols, -1)

    grads_all = jnp.concatenate(grad_blocks, axis=0)
    low_grads = ranks_of(
        lax.dot_general(up, grads_all, (((1,), (1,)), ((), ())), preferred_element_type=F32)
    )
    low_grads = low_grads + jnp.roll(swap(low_grads), planes * tokens, axis=1)
    for bit in bits:
        low_grads = low_grads + flip(low_grads, bit)
    grad_low = (ADAPTER_SCALE * low_grads).astype(BF16)
    wide_gradient = widen(grad_low, own_mask)
    other_gradient = widen(grad_low, other_mask)

    def partial_sum(d):
        gathered = jnp.zeros((tensors, sub, 2 * out_cols), BF16)
        gathered = jnp.concatenate(
            [
                jnp.stack([first[first_order.index(k), d] for k in range(tensors)]),
                jnp.stack([second[second_order.index(k), d] for k in range(tensors)]),
            ],
            axis=1,
        )
        natural = [
            lax.dynamic_index_in_dim(gathered, tensor ^ k, 0, keepdims=False) for k in range(tensors)
        ]
        rows = jnp.concatenate(natural, axis=0)
        here = slice(d * tokens, (d + 1) * tokens)
        return (
            lax.dot_general(rows[:, :out_cols], weight, (((1,), (1,)), ((), ())), preferred_element_type=F32)
            + lax.dot_general(rows[:, out_cols:], other_weight, (((1,), (1,)), ((), ())), preferred_element_type=F32)
            + lax.dot_general(wide_gradient[:, here], down, (((0,), (1,)), ((), ())), preferred_element_type=F32)
            + lax.dot_general(other_gradient[:, here], other_down, (((0,), (1,)), ((), ())), preferred_element_type=F32)
        )

    far = partial_sum(half_ring).astype(BF16)
    back_down, back_up = far[: tokens // 2], far[tokens // 2 :]
    back_down, back_up = send_down(back_down), send_up(back_up)
    for s in range(half_ring - 1, 0, -1):
        mine_down, mine_up = partial_sum(s), partial_sum(planes - s)
        if s == half_ring - 1:
            mine_down = jnp.concatenate(
                [mine_down[: tokens // 2] + back_down.astype(F32), mine_down[tokens // 2 :]], axis=0
            )
            mine_up = jnp.concatenate(
                [mine_up[: tokens // 2], mine_up[tokens // 2 :] + back_up.astype(F32)], axis=0
            )
        else:
            mine_down = mine_down + back_down.astype(F32)
            mine_up = mine_up + back_up.astype(F32)
        back_down, back_up = send_down(mine_down.astype(BF16)), send_up(mine_up.astype(BF16))
    own = partial_sum(0)
    if half_ring > 1:
        total = own + back_down.astype(F32) + back_up.astype(F32)
    else:
        total = own + jnp.concatenate([back_down, back_up], axis=0).astype(F32)
    attention_output_gradient = total.astype(BF16)

    attn_all = jnp.concatenate(attn_blocks, axis=0)
    low_inputs = ranks_of(
        lax.dot_general(down, attn_all, (((0,), (1,)), ((), ())), preferred_element_type=F32)
    )
    for bit in bits:
        low_inputs = low_inputs + flip(low_inputs, bit)
    up_wide = widen((ADAPTER_SCALE * low_inputs).astype(BF16), own_mask)
    down_grad = lax.dot_general(
        attn_all, wide_gradient, (((0,), (1,)), ((), ())), preferred_element_type=F32
    )
    up_grad = jnp.dot(up_wide, grads_all, preferred_element_type=F32)
    return attention_output_gradient, down_grad, up_grad


def solution(mesh):
    placed = (
        P("adapter", "tensor"),
        P(("adapter", "tensor"), None),
        P("adapter"),
        P("tensor", "adapter"),
        P("tensor", "adapter"),
        P("adapter", "tensor"),
    )
    return jax.shard_map(
        per_device,
        mesh=mesh,
        in_specs=placed,
        out_specs=(P("adapter", "tensor"), P("tensor", "adapter"), P("adapter", "tensor")),
        check_vma=False,
    )
```

```python
import functools

import jax
import jax.numpy as jnp
from jax import lax
from jax.experimental import pallas as pl
from jax.experimental.pallas import tpu as pltpu
from jax.sharding import PartitionSpec as P

ADAPTER_RANK = 16
ADAPTER_SCALE = 2.0
ROWS = 16
F32 = jnp.float32
BF16 = jnp.bfloat16
I32 = jnp.int32
NT = (((1,), (1,)), ((), ()))
VMEM_BYTES = 56 * 1024 * 1024
IN_VMEM = pl.BlockSpec(memory_space=pltpu.VMEM)
IN_SMEM = pl.BlockSpec(memory_space=pltpu.SMEM)
ANYWHERE = pl.BlockSpec(memory_space=pl.ANY)


def cost(flops, nbytes):
    return pl.CostEstimate(flops=int(flops) // 64, bytes_accessed=int(nbytes) // 64, transcendentals=0)


def params():
    return pltpu.CompilerParams(vmem_limit_bytes=VMEM_BYTES)


def pack_kernel(slot_ref, *refs):
    pieces, out_ref = refs[:-1], refs[-1]
    shape = (out_ref.shape[0], slot_ref.shape[1])
    pick = (lax.broadcasted_iota(I32, shape, 0) == slot_ref[...]).astype(F32).astype(BF16)
    rows = jnp.concatenate([piece[...] for piece in pieces], axis=0)
    out_ref[...] = jnp.dot(pick, rows, preferred_element_type=F32).astype(BF16)


def pack_rows(slot, pieces, slots):
    tokens, width = slot.shape[1], pieces[0].shape[1]
    tile = min(1024, width)
    column = lambda n: (0, n)
    return pl.pallas_call(
        pack_kernel,
        grid=(width // tile,),
        out_shape=jax.ShapeDtypeStruct((slots, width), BF16),
        in_specs=[pl.BlockSpec((1, tokens), lambda n: (0, 0))]
        + [pl.BlockSpec((piece.shape[0], tile), column) for piece in pieces],
        out_specs=pl.BlockSpec((slots, tile), column),
        compiler_params=params(),
        cost_estimate=cost(2 * tokens * slots * width, 2 * (tokens + slots) * width),
        name="pack_rows",
    )(slot, *pieces)


def masked_sum(projected, local, per_owner):
    total = jnp.zeros((ADAPTER_RANK, projected.shape[1]), F32)
    for j in range(per_owner):
        total = total + jnp.where(local == j, projected[j * ADAPTER_RANK : (j + 1) * ADAPTER_RANK], 0.0)
    return total


def repack_kernel(planes, per_owner, plane_ref, places_ref, local_ref, own_d_ref, other_d_ref, *refs):
    pieces = refs[: 2 * planes - 1]
    own_ref, other_ref, ranks_ref, rows, downs, sems, down_sems = refs[2 * planes - 1 :]
    here, below, above = pieces[0], pieces[1:planes], pieces[planes:]
    plane = plane_ref[0]

    def copy(source, d):
        return pltpu.make_async_copy(source, rows.at[d], sems.at[d])

    copy(here, 0).start()
    for d in range(1, planes):
        @pl.when(plane + d < planes)
        def _():
            copy(below[d - 1], d).start()

        @pl.when(plane + d >= planes)
        def _():
            copy(above[planes - d - 1], d).start()

    weights = [
        pltpu.make_async_copy(source, downs.at[i], down_sems.at[i]) for i, source in enumerate((own_d_ref, other_d_ref))
    ]
    for weight in weights:
        weight.start()
    tokens = here.shape[0]
    capacity = own_ref.shape[0] // planes
    row = lax.broadcasted_iota(I32, (2 * capacity, tokens), 0)
    for d in range(planes):
        copy(here, d).wait()
        pick = (row == places_ref[:, d * tokens : (d + 1) * tokens]).astype(F32).astype(BF16)
        packed = jnp.dot(pick, rows[d], preferred_element_type=F32).astype(BF16)
        own_ref[pl.ds(d * capacity, capacity), :] = packed[:capacity]
        other_ref[pl.ds(d * capacity, capacity), :] = packed[capacity:]
    for i, out_ref in enumerate((own_ref, other_ref)):
        weights[i].wait()
        projected = lax.dot_general(downs[i], out_ref[...], NT, preferred_element_type=F32)
        ranks_ref[i] = masked_sum(projected, local_ref[i : i + 1, :], per_owner)


def repack(plane, places, local, down_ts, here, below, above, capacity, per_owner):
    tokens, width = here.shape
    planes = len(below) + 1
    slots = planes * capacity
    rank_cols = down_ts[0].shape[0]
    return pl.pallas_call(
        functools.partial(repack_kernel, planes, per_owner),
        out_shape=[jax.ShapeDtypeStruct((slots, width), BF16)] * 2
        + [jax.ShapeDtypeStruct((2, ADAPTER_RANK, slots), F32)],
        in_specs=[IN_SMEM, IN_VMEM, IN_VMEM] + [ANYWHERE] * (2 * planes + 1),
        out_specs=[IN_VMEM] * 3,
        scratch_shapes=[
            pltpu.VMEM((planes, tokens, width), BF16),
            pltpu.VMEM((2, rank_cols, width), BF16),
            pltpu.SemaphoreType.DMA((planes,)),
            pltpu.SemaphoreType.DMA((2,)),
        ],
        compiler_params=params(),
        cost_estimate=cost(4 * slots * (tokens + rank_cols) * width, 2 * planes * (tokens + 2 * capacity) * width),
        name="repack",
    )(plane.reshape(1), places, local, *down_ts, here, *below, *above)


def ranks_kernel(per_owner, blocks, order_ref, local_ref, weight_ref, *refs):
    pieces, (out_ref, projected) = refs[:blocks], refs[blocks:]
    k = pl.program_id(0)
    rows = jnp.concatenate([piece[...] for piece in pieces], axis=0)
    part = lax.dot_general(weight_ref[...], rows, NT, preferred_element_type=F32)

    @pl.when(k == 0)
    def _():
        projected[...] = part

    @pl.when(k > 0)
    def _():
        projected[...] += part

    @pl.when(k == pl.num_programs(0) - 1)
    def _():
        out_ref[...] = masked_sum(projected, local_ref[...], per_owner)


def block_specs(blocks, capacity, tile):
    return [pl.BlockSpec((capacity, tile), lambda n, order, i=i: (order[i], n)) for i in range(blocks)]


def token_ranks(order, local, weight, slots, per_owner):
    blocks, width = order.shape[0], weight.shape[1]
    total = local.shape[1]
    rank_cols = weight.shape[0]
    tile = min(512, width)
    return pl.pallas_call(
        functools.partial(ranks_kernel, per_owner, blocks),
        out_shape=jax.ShapeDtypeStruct((ADAPTER_RANK, total), F32),
        grid_spec=pltpu.PrefetchScalarGridSpec(
            num_scalar_prefetch=1,
            grid=(width // tile,),
            in_specs=[
                pl.BlockSpec((1, total), lambda n, order: (0, 0)),
                pl.BlockSpec((rank_cols, tile), lambda n, order: (0, n)),
            ]
            + block_specs(blocks, total // blocks, tile),
            out_specs=pl.BlockSpec((ADAPTER_RANK, total), lambda n, order: (0, 0)),
            scratch_shapes=[pltpu.VMEM((rank_cols, total), F32)],
        ),
        compiler_params=params(),
        cost_estimate=cost(2 * total * width * rank_cols, 2 * width * (total + rank_cols)),
        name="token_ranks",
    )(order, local, weight, *[slots] * blocks)


def load_rows(place_ref, pieces, rows, sems):
    me = place_ref[0]
    copies = []
    tensors = rows.shape[1]
    for i, piece in enumerate(pieces):
        blocks = pl.ds(i // tensors * piece.shape[0], piece.shape[0])
        copies.append(pltpu.make_async_copy(piece, rows.at[blocks, me ^ (i % tensors)], sems.at[i]))
        copies[-1].start()
    for copy in copies:
        copy.wait()


def frozen_kernel(place_ref, own_w_ref, other_w_ref, *refs):
    pieces, (out_ref, rows, sems) = refs[:-3], refs[-3:]
    blocks, tensors, sub, _ = rows.shape
    tokens = tensors * sub
    depth = own_w_ref.shape[1]

    @pl.when(pl.program_id(0) == 0)
    def _():
        load_rows(place_ref, pieces, rows, sems)

    for b in range(blocks):
        x = rows[b].reshape(tokens, 2 * depth)
        product = lax.dot_general(x[:, :depth], own_w_ref[...], NT, preferred_element_type=F32)
        product += lax.dot_general(x[:, depth:], other_w_ref[...], NT, preferred_element_type=F32)
        out_ref[pl.ds(b * tokens, tokens), :] = product


def frozen_part(tensor, weights, pieces):
    blocks, sub, cols = pieces[0].shape
    blocks, tensors = 2 * blocks, len(pieces) // 2
    rows = blocks * sub * tensors
    width, depth = weights[0].shape
    tile = min(512, width)
    return pl.pallas_call(
        frozen_kernel,
        grid=(width // tile,),
        out_shape=jax.ShapeDtypeStruct((rows, width), F32),
        in_specs=[IN_SMEM] + [pl.BlockSpec((tile, depth), lambda n: (n, 0))] * 2 + [ANYWHERE] * len(pieces),
        out_specs=pl.BlockSpec((rows, tile), lambda n: (0, n)),
        scratch_shapes=[pltpu.VMEM((blocks, tensors, sub, cols), BF16), pltpu.SemaphoreType.DMA((len(pieces),))],
        compiler_params=params(),
        cost_estimate=cost(2 * rows * width * cols, 4 * rows * width + 4 * width * depth),
        name="frozen_part",
    )(tensor.reshape(1), *weights, *pieces)


def spread_rows(wide, first, local, ranks, per_owner):
    for j in range(per_owner):
        wide[pl.ds(first + j * ADAPTER_RANK, ADAPTER_RANK), :] = jnp.where(local == j, ranks, 0.0).astype(BF16)


def term_kernel(per_owner, frozen_ref, places_ref, *refs):
    ranks, downs, out_refs, (wide, flat) = refs[:2], refs[2:4], refs[4:-2], refs[-2:]
    rank_cols = downs[0].shape[0]

    @pl.when(pl.program_id(0) == 0)
    def _():
        for i in range(2):
            slot, local = places_ref[i : i + 1, :], places_ref[i + 2 : i + 3, :]
            pick = lax.broadcasted_iota(I32, (ranks[i].shape[1], slot.shape[1]), 0) == slot
            in_order = jnp.dot(ranks[i][...], pick.astype(F32).astype(BF16), preferred_element_type=F32)
            spread_rows(wide, i * rank_cols, local, in_order, per_owner)
        flat[...] = wide[...].T

    total = frozen_ref[...]
    total += jnp.dot(flat[:, :rank_cols], downs[0][...], preferred_element_type=F32)
    total += jnp.dot(flat[:, rank_cols:], downs[1][...], preferred_element_type=F32)
    rows = total.shape[0] // len(out_refs)
    for i, out_ref in enumerate(out_refs):
        out_ref[...] = total[i * rows : (i + 1) * rows].astype(out_ref.dtype)


def add_term(frozen, first, rows, places, ranks, downs, per_owner, types):
    width = frozen.shape[1]
    rank_cols = downs[0].shape[0]
    tile = min(512, width)
    column = lambda n: (0, n)
    each = rows // len(types)
    return pl.pallas_call(
        functools.partial(term_kernel, per_owner),
        grid=(width // tile,),
        out_shape=[jax.ShapeDtypeStruct((each, width), kind) for kind in types],
        in_specs=[
            pl.BlockSpec((rows, tile), lambda n: (first, n)),
            pl.BlockSpec((places.shape[0], rows), lambda n: (0, first)),
        ]
        + [pl.BlockSpec(x.shape, lambda n: (0, 0)) for x in ranks]
        + [pl.BlockSpec((rank_cols, tile), column)] * 2,
        out_specs=[pl.BlockSpec((each, tile), column)] * len(types),
        scratch_shapes=[pltpu.VMEM((2 * rank_cols, rows), BF16), pltpu.VMEM((rows, 2 * rank_cols), BF16)],
        compiler_params=params(),
        cost_estimate=cost(4 * rows * width * rank_cols, 6 * rows * width + 4 * rank_cols * width),
        name="add_term",
    )(frozen, places, *ranks, *downs)


def gradients_kernel(per_owner, blocks, order_ref, local_ref, grad_ranks_ref, up_ranks_ref, own_ref, other_ref, *refs):
    grad, (down_ref, up_ref, wide_grad, wide_up) = refs[:blocks], refs[blocks:]

    @pl.when(pl.program_id(0) == 0)
    def _():
        local = local_ref[...]
        spread_rows(wide_grad, 0, local, grad_ranks_ref[...].astype(F32), per_owner)
        spread_rows(wide_up, 0, local, up_ranks_ref[...].astype(F32), per_owner)

    rows = jnp.concatenate([own_ref[...], other_ref[...]], axis=0)
    down_ref[...] = jnp.dot(wide_grad[...], rows, preferred_element_type=F32).T
    rows = jnp.concatenate([piece[...] for piece in grad], axis=0)
    up_ref[...] = jnp.dot(wide_up[...], rows, preferred_element_type=F32)


def adapter_gradients(order, local, grad_ranks, up_ranks, attn, grad, per_owner):
    total, width = grad.shape
    blocks = order.shape[0]
    rank_cols = per_owner * ADAPTER_RANK
    tile = min(256, width)
    whole = lambda n, order: (0, 0)
    column = lambda n, order: (0, n)
    return pl.pallas_call(
        functools.partial(gradients_kernel, per_owner, blocks),
        out_shape=(
            jax.ShapeDtypeStruct((width, rank_cols), F32),
            jax.ShapeDtypeStruct((rank_cols, width), F32),
        ),
        grid_spec=pltpu.PrefetchScalarGridSpec(
            num_scalar_prefetch=1,
            grid=(width // tile,),
            in_specs=[pl.BlockSpec((1, total), whole)]
            + [pl.BlockSpec((ADAPTER_RANK, total), whole)] * 2
            + [pl.BlockSpec((total // 2, tile), column)] * 2
            + block_specs(blocks, total // blocks, tile),
            out_specs=(
                pl.BlockSpec((tile, rank_cols), lambda n, order: (n, 0)),
                pl.BlockSpec((rank_cols, tile), column),
            ),
            scratch_shapes=[pltpu.VMEM((rank_cols, total), BF16)] * 2,
        ),
        compiler_params=params(),
        cost_estimate=cost(4 * total * width * rank_cols, 4 * total * width + 8 * rank_cols * width),
        name="adapter_gradients",
    )(order, local, grad_ranks, up_ranks, *attn, *[grad] * blocks)


def per_device(attn, grad, ids, weight, down, up):
    owners = lax.axis_size("adapter")
    tensors = lax.axis_size("tensor")
    planes = owners // 2
    me = lax.axis_index("adapter")
    plane, core = me // 2, me % 2
    tensor = lax.axis_index("tensor")
    tokens, width = attn.shape
    sub = grad.shape[0]
    out_cols = weight.shape[1]
    rank_cols = down.shape[1]
    per_owner = rank_cols // ADAPTER_RANK
    capacity = -(-5 * tokens // (2 * owners) // ROWS) * ROWS
    slot_count = owners * capacity

    def shift(x, by):
        pairs = [(2 * z + c, 2 * ((z + by) % planes) + c) for z in range(planes) for c in range(2)]
        return lax.ppermute(x, "adapter", pairs)

    def up_line(x, distance):
        pairs = [(2 * z + c, 2 * z + 2 + c) for z in range(planes - distance) for c in range(2)]
        return lax.ppermute(x, "adapter", pairs)

    def down_line(x, distance):
        pairs = [(2 * z + c, 2 * z - 2 + c) for z in range(distance, planes) for c in range(2)]
        return lax.ppermute(x, "adapter", pairs)

    def attn_line(x, d, way):
        planes_on = range(d - 1, planes - 1) if way == 1 else range(1, planes - d + 1)
        return lax.ppermute(x, "adapter", [(2 * z + c, 2 * (z + way) + c) for z in planes_on for c in range(2)])

    def swap(x):
        return lax.ppermute(x, "adapter", [(a, a ^ 1) for a in range(owners)])

    def flip(x, k):
        return lax.ppermute(x, "tensor", [(t, t ^ k) for t in range(tensors)])

    def after(x, *others):
        return lax.optimization_barrier((x, *others))[0]

    def tensor_cols(k):
        return lax.dynamic_slice_in_dim(grad, (tensor ^ k) * width, width, 1)

    tensor_parts = [tensor_cols(k) for k in range(tensors)]
    grad_rows = tensor_parts[:1] + [flip(tensor_parts[k], k) for k in range(1, tensors)]
    grad_again, ids_again = after((grad, ids), *tensor_parts)

    def plane_cols(offset):
        p = (plane + offset) % planes
        parts = [
            lax.dynamic_slice_in_dim(grad_again, (2 * p + c) * out_cols, out_cols, 1) for c in (core, 1 - core)
        ]
        return jnp.concatenate(parts, axis=1)

    half = planes // 2
    order = [d for s in range(1, half) for d in (s, planes - s)] + [half, 0]
    plane_parts = [plane_cols(d) for d in range(planes)]
    part = {0: plane_parts[0]}
    for d in range(1, planes):
        part[planes - d] = shift(plane_parts[d], d)
    ids_again = after(ids_again, *plane_parts)

    all_ids = lax.all_to_all(jnp.broadcast_to(ids_again, (owners, tokens)), "adapter", 0, 0, tiled=True)

    def placing(block_ids):
        owner = block_ids // per_owner
        earlier = jnp.arange(tokens)[:, None] > jnp.arange(tokens)[None, :]
        same = owner[..., :, None] == owner[..., None, :]
        place = jnp.sum((same & earlier).astype(I32), axis=-1)
        return owner, place

    owner, place = placing(ids)
    slot = owner * capacity + place
    slot_here = jnp.concatenate(
        [lax.dynamic_slice_in_dim(slot, (tensor ^ k) * sub, sub, 0) for k in range(tensors)]
    )
    down_t = down.T
    grad_packed = pack_rows(slot_here.reshape(1, -1), after(grad_rows, down_t), slot_count)

    def to_owners(x):
        x = x.reshape(owners, capacity, width)
        return lax.all_to_all(x, "adapter", 0, 0, tiled=True).reshape(slot_count, width)

    grad_packed = after(grad_packed, *(part[d] for d in range(1, planes)))
    grad_slots = to_owners(grad_packed)

    halves = [jnp.stack([part[d] for d in order[i * half : (i + 1) * half]], axis=0) for i in range(2)]
    bits = [1 << i for i in range(tensors.bit_length() - 1)]
    plane_rows = [{0: halves[0]}, {0: halves[1]}]
    for step in zip(bits, reversed(bits)):
        for rows, bit in zip(plane_rows, step):
            rows.update({k ^ bit: flip(x, bit) for k, x in list(rows.items())})
    plane_rows = [rows[k] for rows in plane_rows for k in range(tensors)]
    other_weight = swap(weight)
    other_down_t = swap(down_t)

    all_owner, all_place = placing(all_ids)
    ahead = [2 * ((plane + jnp.arange(planes)) % planes) + c for c in (core, 1 - core)]
    slot_order = jnp.concatenate(ahead)

    def labels(owner, blocks):
        mine = (all_owner[blocks] == owner)[:, None, :]
        mine &= all_place[blocks][:, None, :] == jnp.arange(capacity, dtype=I32)[:, None]
        from_first = all_ids[blocks][:, None, :] - owner * per_owner
        return (jnp.sum(jnp.where(mine, from_first + 1, 0), axis=-1) - 1).reshape(1, -1)

    here, there = (labels(me, blocks) for blocks in ahead)
    local = jnp.concatenate([here, there], axis=1)
    parity_local = jnp.concatenate([here, labels(me ^ 1, ahead[0])], axis=0)

    parity_ids, parity_owner, parity_place = (x[ahead[0]] for x in (all_ids, all_owner, all_place))
    attn_places = jnp.where(parity_owner == me, parity_place, -1)
    attn_places = jnp.where(parity_owner == (me ^ 1), parity_place + capacity, attn_places).reshape(1, -1)
    base = capacity * jnp.arange(planes, dtype=I32)[:, None]
    places = jnp.stack(
        [
            jnp.where(parity_owner == me, parity_place + base, -1),
            jnp.where(parity_owner == (me ^ 1), parity_place + base + planes * capacity, -1),
            parity_ids - me * per_owner,
            parity_ids - (me ^ 1) * per_owner,
        ]
    )
    places = jnp.concatenate([places[:, d : d + 1] for d in order], axis=1).reshape(4, -1)

    first_weight = after(weight, places, local, parity_local, attn_places, slot_order, other_down_t)
    attn_start = after(attn, *plane_rows)
    going_down, going_up = attn_line(attn_start, 1, -1), attn_line(attn_start, 1, 1)
    frozen = frozen_part(tensor, (first_weight, other_weight), plane_rows)
    grad_slots = after(grad_slots, frozen)
    low_grads = token_ranks(slot_order, local, up, grad_slots, per_owner)
    low_grads = sum([flip(low_grads, k) for k in range(1, tensors)], low_grads)
    grad_low = (ADAPTER_SCALE * low_grads).astype(BF16)
    ranks = (grad_low, swap(grad_low))
    downs = (down_t, other_down_t)

    def with_term(i, types):
        return add_term(frozen, i, half * tokens, places, ranks, downs, per_owner, types)

    pairs = with_term(0, [BF16] * planes)
    below, above = [going_down], [going_up]
    for d in range(2, planes):
        if d == 2:
            going_down, going_up = after((going_down, going_up), *pairs)
        going_down, going_up = attn_line(going_down, d, -1), attn_line(going_up, d, 1)
        below.append(going_down)
        above.append(going_up)
    pairs += with_term(1, [BF16] * (planes - 2) + [F32] * 2)
    sums = {d: pairs[2 * i : 2 * i + 2] for i, d in enumerate(order)}
    attn_own, attn_other, parity_inputs = repack(
        plane, attn_places, parity_local, downs, attn, below, above, capacity, per_owner
    )
    attn_slots = [attn_own, swap(attn_other)]
    going_up, going_down = [None, None], [None, None]
    for d in range(planes - 1, 0, -1):
        for i in range(2):
            up_sum, down_sum = sums[d][i], sums[planes - d][i]
            if d == 1 and i == 1:
                up_sum, down_sum = after((up_sum, down_sum), parity_inputs)
            if going_up[i] is not None:
                up_sum = (up_sum.astype(F32) + going_up[i].astype(F32)).astype(BF16)
                down_sum = (down_sum.astype(F32) + going_down[i].astype(F32)).astype(BF16)
            going_up[i], going_down[i] = up_line(up_sum, d), down_line(down_sum, d)
    total = [x + up_sum.astype(F32) + down_sum.astype(F32) for x, up_sum, down_sum in zip(sums[0], going_up, going_down)]
    attention_output_gradient = jnp.concatenate(total, axis=0).astype(BF16)

    low_inputs = sum([flip(parity_inputs, k) for k in range(1, tensors)], parity_inputs)
    up_scaled = (ADAPTER_SCALE * low_inputs).astype(BF16)
    up_scaled = jnp.concatenate([up_scaled[0], swap(up_scaled[1])], axis=1)
    down_grad, up_grad = adapter_gradients(slot_order, local, grad_low, up_scaled, attn_slots, grad_slots, per_owner)
    return attention_output_gradient, down_grad, up_grad


def solution(mesh):
    placed = (
        P("adapter", "tensor"),
        P(("adapter", "tensor"), None),
        P("adapter"),
        P("tensor", "adapter"),
        P("tensor", "adapter"),
        P("adapter", "tensor"),
    )
    return jax.shard_map(
        per_device,
        mesh=mesh,
        in_specs=placed,
        out_specs=(P("adapter", "tensor"), P("tensor", "adapter"), P("adapter", "tensor")),
        check_vma=False,
    )
```

```python
import functools

import jax
import jax.numpy as jnp
from jax import lax
from jax.experimental import pallas as pl
from jax.experimental.pallas import tpu as pltpu
from jax.sharding import PartitionSpec as P

ADAPTER_RANK = 16
ADAPTER_SCALE = 2.0
ROWS = 16
F32 = jnp.float32
BF16 = jnp.bfloat16
I32 = jnp.int32
NT = (((1,), (1,)), ((), ()))
VMEM_BYTES = 56 * 1024 * 1024
IN_VMEM = pl.BlockSpec(memory_space=pltpu.VMEM)
IN_SMEM = pl.BlockSpec(memory_space=pltpu.SMEM)
ANYWHERE = pl.BlockSpec(memory_space=pl.ANY)


def cost(flops, nbytes):
    return pl.CostEstimate(flops=int(flops) // 64, bytes_accessed=int(nbytes) // 64, transcendentals=0)


def params():
    return pltpu.CompilerParams(vmem_limit_bytes=VMEM_BYTES)


def pack_kernel(slot_ref, *refs):
    pieces, out_ref = refs[:-1], refs[-1]
    shape = (out_ref.shape[0], slot_ref.shape[1])
    pick = (lax.broadcasted_iota(I32, shape, 0) == slot_ref[...]).astype(F32).astype(BF16)
    rows = jnp.concatenate([piece[...] for piece in pieces], axis=0)
    out_ref[...] = jnp.dot(pick, rows, preferred_element_type=F32).astype(BF16)


def pack_rows(slot, pieces, slots):
    tokens, width = slot.shape[1], pieces[0].shape[1]
    tile = min(1024, width)
    column = lambda n: (0, n)
    return pl.pallas_call(
        pack_kernel,
        grid=(width // tile,),
        out_shape=jax.ShapeDtypeStruct((slots, width), BF16),
        in_specs=[pl.BlockSpec((1, tokens), lambda n: (0, 0))]
        + [pl.BlockSpec((piece.shape[0], tile), column) for piece in pieces],
        out_specs=pl.BlockSpec((slots, tile), column),
        compiler_params=params(),
        cost_estimate=cost(2 * tokens * slots * width, 2 * (tokens + slots) * width),
        name="pack_rows",
    )(slot, *pieces)


def masked_sum(projected, local, per_owner):
    total = jnp.zeros((ADAPTER_RANK, projected.shape[1]), F32)
    for j in range(per_owner):
        total = total + jnp.where(local == j, projected[j * ADAPTER_RANK : (j + 1) * ADAPTER_RANK], 0.0)
    return total


def repack_kernel(planes, per_owner, plane_ref, places_ref, local_ref, own_d_ref, other_d_ref, *refs):
    pieces = refs[: 2 * planes - 1]
    own_ref, other_ref, ranks_ref, rows, downs, sems, down_sems = refs[2 * planes - 1 :]
    here, below, above = pieces[0], pieces[1:planes], pieces[planes:]
    plane = plane_ref[0]

    def copy(source, d):
        return pltpu.make_async_copy(source, rows.at[d], sems.at[d])

    copy(here, 0).start()
    for d in range(1, planes):
        @pl.when(plane + d < planes)
        def _():
            copy(below[d - 1], d).start()

        @pl.when(plane + d >= planes)
        def _():
            copy(above[planes - d - 1], d).start()

    weights = [
        pltpu.make_async_copy(source, downs.at[i], down_sems.at[i]) for i, source in enumerate((own_d_ref, other_d_ref))
    ]
    for weight in weights:
        weight.start()
    tokens = here.shape[0]
    capacity = own_ref.shape[0] // planes
    row = lax.broadcasted_iota(I32, (2 * capacity, tokens), 0)
    for d in range(planes):
        copy(here, d).wait()
        pick = (row == places_ref[:, d * tokens : (d + 1) * tokens]).astype(F32).astype(BF16)
        packed = jnp.dot(pick, rows[d], preferred_element_type=F32).astype(BF16)
        own_ref[pl.ds(d * capacity, capacity), :] = packed[:capacity]
        other_ref[pl.ds(d * capacity, capacity), :] = packed[capacity:]
    for i, out_ref in enumerate((own_ref, other_ref)):
        weights[i].wait()
        projected = lax.dot_general(downs[i], out_ref[...], NT, preferred_element_type=F32)
        ranks_ref[i] = masked_sum(projected, local_ref[i : i + 1, :], per_owner)


def repack(plane, places, local, down_ts, here, below, above, capacity, per_owner):
    tokens, width = here.shape
    planes = len(below) + 1
    slots = planes * capacity
    rank_cols = down_ts[0].shape[0]
    return pl.pallas_call(
        functools.partial(repack_kernel, planes, per_owner),
        out_shape=[jax.ShapeDtypeStruct((slots, width), BF16)] * 2
        + [jax.ShapeDtypeStruct((2, ADAPTER_RANK, slots), F32)],
        in_specs=[IN_SMEM, IN_VMEM, IN_VMEM] + [ANYWHERE] * (2 * planes + 1),
        out_specs=[IN_VMEM] * 3,
        scratch_shapes=[
            pltpu.VMEM((planes, tokens, width), BF16),
            pltpu.VMEM((2, rank_cols, width), BF16),
            pltpu.SemaphoreType.DMA((planes,)),
            pltpu.SemaphoreType.DMA((2,)),
        ],
        compiler_params=params(),
        cost_estimate=cost(4 * slots * (tokens + rank_cols) * width, 2 * planes * (tokens + 2 * capacity) * width),
        name="repack",
    )(plane.reshape(1), places, local, *down_ts, here, *below, *above)


def ranks_kernel(per_owner, blocks, order_ref, local_ref, weight_ref, *refs):
    pieces, (out_ref, projected) = refs[:blocks], refs[blocks:]
    k = pl.program_id(0)
    rows = jnp.concatenate([piece[...] for piece in pieces], axis=0)
    part = lax.dot_general(weight_ref[...], rows, NT, preferred_element_type=F32)

    @pl.when(k == 0)
    def _():
        projected[...] = part

    @pl.when(k > 0)
    def _():
        projected[...] += part

    @pl.when(k == pl.num_programs(0) - 1)
    def _():
        out_ref[...] = masked_sum(projected, local_ref[...], per_owner)


def block_specs(blocks, capacity, tile):
    return [pl.BlockSpec((capacity, tile), lambda n, order, i=i: (order[i], n)) for i in range(blocks)]


def token_ranks(order, local, weight, slots, per_owner):
    blocks, width = order.shape[0], weight.shape[1]
    total = local.shape[1]
    rank_cols = weight.shape[0]
    tile = min(512, width)
    return pl.pallas_call(
        functools.partial(ranks_kernel, per_owner, blocks),
        out_shape=jax.ShapeDtypeStruct((ADAPTER_RANK, total), F32),
        grid_spec=pltpu.PrefetchScalarGridSpec(
            num_scalar_prefetch=1,
            grid=(width // tile,),
            in_specs=[
                pl.BlockSpec((1, total), lambda n, order: (0, 0)),
                pl.BlockSpec((rank_cols, tile), lambda n, order: (0, n)),
            ]
            + block_specs(blocks, total // blocks, tile),
            out_specs=pl.BlockSpec((ADAPTER_RANK, total), lambda n, order: (0, 0)),
            scratch_shapes=[pltpu.VMEM((rank_cols, total), F32)],
        ),
        compiler_params=params(),
        cost_estimate=cost(2 * total * width * rank_cols, 2 * width * (total + rank_cols)),
        name="token_ranks",
    )(order, local, weight, *[slots] * blocks)


def load_rows(names, place_ref, pieces, rows, sems):
    me = place_ref[0]
    copies = []
    for (first, ks), piece in zip(names, pieces):
        blocks = pl.ds(first, piece.shape[1])
        for j, k in enumerate(ks):
            copies.append(pltpu.make_async_copy(piece.at[j], rows.at[blocks, me ^ k], sems.at[len(copies)]))
            copies[-1].start()
    for copy in copies:
        copy.wait()


def frozen_kernel(names, place_ref, own_w_ref, other_w_ref, *refs):
    pieces, (out_ref, rows, sems) = refs[:-3], refs[-3:]
    blocks, tensors, sub, _ = rows.shape
    tokens = tensors * sub
    depth = own_w_ref.shape[1]

    @pl.when(pl.program_id(0) == 0)
    def _():
        load_rows(names, place_ref, pieces, rows, sems)

    for b in range(blocks):
        x = rows[b].reshape(tokens, 2 * depth)
        product = lax.dot_general(x[:, :depth], own_w_ref[...], NT, preferred_element_type=F32)
        product += lax.dot_general(x[:, depth:], other_w_ref[...], NT, preferred_element_type=F32)
        out_ref[pl.ds(b * tokens, tokens), :] = product


def frozen_part(tensor, weights, names, pieces):
    _, blocks, sub, cols = pieces[0].shape
    blocks, tensors = 2 * blocks, sum(len(ks) for _, ks in names) // 2
    rows = blocks * sub * tensors
    width, depth = weights[0].shape
    tile = min(512, width)
    return pl.pallas_call(
        functools.partial(frozen_kernel, names),
        grid=(width // tile,),
        out_shape=jax.ShapeDtypeStruct((rows, width), F32),
        in_specs=[IN_SMEM] + [pl.BlockSpec((tile, depth), lambda n: (n, 0))] * 2 + [ANYWHERE] * len(pieces),
        out_specs=pl.BlockSpec((rows, tile), lambda n: (0, n)),
        scratch_shapes=[pltpu.VMEM((blocks, tensors, sub, cols), BF16), pltpu.SemaphoreType.DMA((2 * tensors,))],
        compiler_params=params(),
        cost_estimate=cost(2 * rows * width * cols, 4 * rows * width + 4 * width * depth),
        name="frozen_part",
    )(tensor.reshape(1), *weights, *pieces)


def spread_rows(wide, first, local, ranks, per_owner):
    for j in range(per_owner):
        wide[pl.ds(first + j * ADAPTER_RANK, ADAPTER_RANK), :] = jnp.where(local == j, ranks, 0.0).astype(BF16)


def term_kernel(per_owner, frozen_ref, places_ref, *refs):
    ranks, downs, out_refs, (wide, flat) = refs[:2], refs[2:4], refs[4:-2], refs[-2:]
    rank_cols = downs[0].shape[0]

    @pl.when(pl.program_id(0) == 0)
    def _():
        for i in range(2):
            slot, local = places_ref[i : i + 1, :], places_ref[i + 2 : i + 3, :]
            pick = lax.broadcasted_iota(I32, (ranks[i].shape[1], slot.shape[1]), 0) == slot
            in_order = jnp.dot(ranks[i][...], pick.astype(F32).astype(BF16), preferred_element_type=F32)
            spread_rows(wide, i * rank_cols, local, in_order, per_owner)
        flat[...] = wide[...].T

    total = frozen_ref[...]
    total += jnp.dot(flat[:, :rank_cols], downs[0][...], preferred_element_type=F32)
    total += jnp.dot(flat[:, rank_cols:], downs[1][...], preferred_element_type=F32)
    rows = total.shape[0] // len(out_refs)
    for i, out_ref in enumerate(out_refs):
        out_ref[...] = total[i * rows : (i + 1) * rows].astype(out_ref.dtype)


def add_term(frozen, first, rows, places, ranks, downs, per_owner, types):
    width = frozen.shape[1]
    rank_cols = downs[0].shape[0]
    tile = min(512, width)
    column = lambda n: (0, n)
    each = rows // len(types)
    return pl.pallas_call(
        functools.partial(term_kernel, per_owner),
        grid=(width // tile,),
        out_shape=[jax.ShapeDtypeStruct((each, width), kind) for kind in types],
        in_specs=[
            pl.BlockSpec((rows, tile), lambda n: (first, n)),
            pl.BlockSpec((places.shape[0], rows), lambda n: (0, first)),
        ]
        + [pl.BlockSpec(x.shape, lambda n: (0, 0)) for x in ranks]
        + [pl.BlockSpec((rank_cols, tile), column)] * 2,
        out_specs=[pl.BlockSpec((each, tile), column)] * len(types),
        scratch_shapes=[pltpu.VMEM((2 * rank_cols, rows), BF16), pltpu.VMEM((rows, 2 * rank_cols), BF16)],
        compiler_params=params(),
        cost_estimate=cost(4 * rows * width * rank_cols, 6 * rows * width + 4 * rank_cols * width),
        name="add_term",
    )(frozen, places, *ranks, *downs)


def gradients_kernel(per_owner, blocks, order_ref, local_ref, grad_ranks_ref, up_ranks_ref, own_ref, other_ref, *refs):
    grad, (down_ref, up_ref, wide_grad, wide_up) = refs[:blocks], refs[blocks:]

    @pl.when(pl.program_id(0) == 0)
    def _():
        local = local_ref[...]
        spread_rows(wide_grad, 0, local, grad_ranks_ref[...].astype(F32), per_owner)
        spread_rows(wide_up, 0, local, up_ranks_ref[...].astype(F32), per_owner)

    rows = jnp.concatenate([own_ref[...], other_ref[...]], axis=0)
    down_ref[...] = jnp.dot(wide_grad[...], rows, preferred_element_type=F32).T
    rows = jnp.concatenate([piece[...] for piece in grad], axis=0)
    up_ref[...] = jnp.dot(wide_up[...], rows, preferred_element_type=F32)


def adapter_gradients(order, local, grad_ranks, up_ranks, attn, grad, per_owner):
    total, width = grad.shape
    blocks = order.shape[0]
    rank_cols = per_owner * ADAPTER_RANK
    tile = min(256, width)
    whole = lambda n, order: (0, 0)
    column = lambda n, order: (0, n)
    return pl.pallas_call(
        functools.partial(gradients_kernel, per_owner, blocks),
        out_shape=(
            jax.ShapeDtypeStruct((width, rank_cols), F32),
            jax.ShapeDtypeStruct((rank_cols, width), F32),
        ),
        grid_spec=pltpu.PrefetchScalarGridSpec(
            num_scalar_prefetch=1,
            grid=(width // tile,),
            in_specs=[pl.BlockSpec((1, total), whole)]
            + [pl.BlockSpec((ADAPTER_RANK, total), whole)] * 2
            + [pl.BlockSpec((total // 2, tile), column)] * 2
            + block_specs(blocks, total // blocks, tile),
            out_specs=(
                pl.BlockSpec((tile, rank_cols), lambda n, order: (n, 0)),
                pl.BlockSpec((rank_cols, tile), column),
            ),
            scratch_shapes=[pltpu.VMEM((rank_cols, total), BF16)] * 2,
        ),
        compiler_params=params(),
        cost_estimate=cost(4 * total * width * rank_cols, 4 * total * width + 8 * rank_cols * width),
        name="adapter_gradients",
    )(order, local, grad_ranks, up_ranks, *attn, *[grad] * blocks)


def per_device(attn, grad, ids, weight, down, up):
    owners = lax.axis_size("adapter")
    tensors = lax.axis_size("tensor")
    planes = owners // 2
    me = lax.axis_index("adapter")
    plane, core = me // 2, me % 2
    tensor = lax.axis_index("tensor")
    tokens, width = attn.shape
    sub = grad.shape[0]
    out_cols = weight.shape[1]
    rank_cols = down.shape[1]
    per_owner = rank_cols // ADAPTER_RANK
    capacity = -(-5 * tokens // (2 * owners) // ROWS) * ROWS
    slot_count = owners * capacity

    def shift(x, by):
        pairs = [(2 * z + c, 2 * ((z + by) % planes) + c) for z in range(planes) for c in range(2)]
        return lax.ppermute(x, "adapter", pairs)

    def up_line(x, distance):
        pairs = [(2 * z + c, 2 * z + 2 + c) for z in range(planes - distance) for c in range(2)]
        return lax.ppermute(x, "adapter", pairs)

    def down_line(x, distance):
        pairs = [(2 * z + c, 2 * z - 2 + c) for z in range(distance, planes) for c in range(2)]
        return lax.ppermute(x, "adapter", pairs)

    def attn_line(x, d, way):
        planes_on = range(d - 1, planes - 1) if way == 1 else range(1, planes - d + 1)
        return lax.ppermute(x, "adapter", [(2 * z + c, 2 * (z + way) + c) for z in planes_on for c in range(2)])

    def swap(x):
        return lax.ppermute(x, "adapter", [(a, a ^ 1) for a in range(owners)])

    def flip(x, k):
        return lax.ppermute(x, "tensor", [(t, t ^ k) for t in range(tensors)])

    def after(x, *others):
        return lax.optimization_barrier((x, *others))[0]

    def tensor_cols(k):
        return lax.dynamic_slice_in_dim(grad, (tensor ^ k) * width, width, 1)

    tensor_parts = [tensor_cols(k) for k in range(tensors)]
    grad_rows = tensor_parts[:1] + [flip(tensor_parts[k], k) for k in range(1, tensors)]
    grad_again, ids_again = after((grad, ids), *tensor_parts)

    def plane_cols(offset):
        p = (plane + offset) % planes
        parts = [
            lax.dynamic_slice_in_dim(grad_again, (2 * p + c) * out_cols, out_cols, 1) for c in (core, 1 - core)
        ]
        return jnp.concatenate(parts, axis=1)

    half = planes // 2
    order = [d for s in range(1, half) for d in (s, planes - s)] + [half, 0]
    plane_parts = [plane_cols(d) for d in range(planes)]
    part = {0: plane_parts[0]}
    for d in range(1, planes):
        part[planes - d] = shift(plane_parts[d], d)
    ids_again = after(ids_again, *plane_parts, *grad_rows[1:])

    all_ids = lax.all_to_all(jnp.broadcast_to(ids_again, (owners, tokens)), "adapter", 0, 0, tiled=True)

    def placing(block_ids):
        owner = block_ids // per_owner
        earlier = jnp.arange(tokens)[:, None] > jnp.arange(tokens)[None, :]
        same = owner[..., :, None] == owner[..., None, :]
        place = jnp.sum((same & earlier).astype(I32), axis=-1)
        return owner, place

    owner, place = placing(ids)
    slot = owner * capacity + place
    slot_here = jnp.concatenate(
        [lax.dynamic_slice_in_dim(slot, (tensor ^ k) * sub, sub, 0) for k in range(tensors)]
    )
    down_t = down.T
    grad_packed = pack_rows(slot_here.reshape(1, -1), after(grad_rows, down_t), slot_count)

    def to_owners(x):
        x = x.reshape(owners, capacity, width)
        return lax.all_to_all(x, "adapter", 0, 0, tiled=True).reshape(slot_count, width)

    grad_packed = after(grad_packed, *(part[d] for d in range(1, planes)))
    grad_slots = to_owners(grad_packed)

    halves = [jnp.stack([part[d] for d in order[i * half : (i + 1) * half]], axis=0) for i in range(2)]
    bits = [1 << i for i in range(tensors.bit_length() - 1)]
    plane_rows = [[([0], x[None])] for x in halves]
    for step in zip(bits, reversed(bits)):
        for rows, bit in zip(plane_rows, step):
            sent = jnp.concatenate([x for _, x in rows], axis=0) if len(rows) > 1 else rows[0][1]
            rows.append(([k ^ bit for ks, _ in rows for k in ks], flip(sent, bit)))
    first_rows = [rows[1][1] for rows in plane_rows]
    row_names = [(i * half, ks) for i, rows in enumerate(plane_rows) for ks, _ in rows]
    plane_rows = [x for rows in plane_rows for _, x in rows]
    all_ids = after(all_ids, *first_rows)
    other_weight = swap(weight)
    other_down_t = swap(down_t)

    all_owner, all_place = placing(all_ids)
    ahead = [2 * ((plane + jnp.arange(planes)) % planes) + c for c in (core, 1 - core)]
    slot_order = jnp.concatenate(ahead)

    def labels(owner, blocks):
        mine = (all_owner[blocks] == owner)[:, None, :]
        mine &= all_place[blocks][:, None, :] == jnp.arange(capacity, dtype=I32)[:, None]
        from_first = all_ids[blocks][:, None, :] - owner * per_owner
        return (jnp.sum(jnp.where(mine, from_first + 1, 0), axis=-1) - 1).reshape(1, -1)

    here, there = (labels(me, blocks) for blocks in ahead)
    local = jnp.concatenate([here, there], axis=1)
    parity_local = jnp.concatenate([here, labels(me ^ 1, ahead[0])], axis=0)

    parity_ids, parity_owner, parity_place = (x[ahead[0]] for x in (all_ids, all_owner, all_place))
    attn_places = jnp.where(parity_owner == me, parity_place, -1)
    attn_places = jnp.where(parity_owner == (me ^ 1), parity_place + capacity, attn_places).reshape(1, -1)
    base = capacity * jnp.arange(planes, dtype=I32)[:, None]
    places = jnp.stack(
        [
            jnp.where(parity_owner == me, parity_place + base, -1),
            jnp.where(parity_owner == (me ^ 1), parity_place + base + planes * capacity, -1),
            parity_ids - me * per_owner,
            parity_ids - (me ^ 1) * per_owner,
        ]
    )
    places = jnp.concatenate([places[:, d : d + 1] for d in order], axis=1).reshape(4, -1)

    first_weight = after(weight, places, local, parity_local, attn_places, slot_order, other_down_t)
    attn_start = after(attn, *first_rows)
    going_down, going_up = attn_line(attn_start, 1, -1), attn_line(attn_start, 1, 1)
    frozen = frozen_part(tensor, (first_weight, other_weight), row_names, plane_rows)
    grad_slots = after(grad_slots, frozen)
    part_grads = token_ranks(slot_order, local, up, grad_slots, per_owner)
    low_grads = sum([flip(part_grads, k) for k in range(1, tensors)], part_grads)
    grad_low = (ADAPTER_SCALE * low_grads).astype(BF16)
    ranks = (grad_low, swap(grad_low))
    downs = (down_t, other_down_t)

    def with_term(i, types):
        return add_term(frozen, i, half * tokens, places, ranks, downs, per_owner, types)

    pairs = with_term(0, [BF16] * planes)
    below, above = [going_down], [going_up]
    for d in range(2, planes):
        if d == 2:
            going_down, going_up = after((going_down, going_up), part_grads)
        going_down, going_up = attn_line(going_down, d, -1), attn_line(going_up, d, 1)
        below.append(going_down)
        above.append(going_up)
    pairs += with_term(1, [BF16] * (planes - 2) + [F32] * 2)
    sums = {d: pairs[2 * i : 2 * i + 2] for i, d in enumerate(order)}
    going_up, going_down = [None, None], [None, None]
    for d in range(planes - 1, 0, -1):
        for i in range(2):
            up_sum, down_sum = sums[d][i], sums[planes - d][i]
            if d == planes - 2 and i == 0:
                up_sum, down_sum = after((up_sum, down_sum), below[1], above[1])
            if going_up[i] is not None:
                up_sum = (up_sum.astype(F32) + going_up[i].astype(F32)).astype(BF16)
                down_sum = (down_sum.astype(F32) + going_down[i].astype(F32)).astype(BF16)
            last_sums = (up_sum, down_sum)
            going_up[i], going_down[i] = up_line(up_sum, d), down_line(down_sum, d)
    below[-1], above[-1] = after((below[-1], above[-1]), *last_sums)
    attn_own, attn_other, parity_inputs = repack(
        plane, attn_places, parity_local, downs, attn, below, above, capacity, per_owner
    )
    attn_slots = [attn_own, swap(attn_other)]
    low_inputs = sum([flip(parity_inputs, k) for k in range(1, tensors)], parity_inputs)
    up_scaled = (ADAPTER_SCALE * low_inputs).astype(BF16)
    up_scaled = jnp.concatenate([up_scaled[0], swap(up_scaled[1])], axis=1)
    down_grad, up_grad = adapter_gradients(slot_order, local, grad_low, up_scaled, attn_slots, grad_slots, per_owner)
    going_up, going_down = after((going_up, going_down), down_grad)
    total = [x + up_sum.astype(F32) + down_sum.astype(F32) for x, up_sum, down_sum in zip(sums[0], going_up, going_down)]
    attention_output_gradient = jnp.concatenate(total, axis=0).astype(BF16)
    return attention_output_gradient, down_grad, up_grad


def solution(mesh):
    placed = (
        P("adapter", "tensor"),
        P(("adapter", "tensor"), None),
        P("adapter"),
        P("tensor", "adapter"),
        P("tensor", "adapter"),
        P("adapter", "tensor"),
    )
    return jax.shard_map(
        per_device,
        mesh=mesh,
        in_specs=placed,
        out_specs=(P("adapter", "tensor"), P("tensor", "adapter"), P("adapter", "tensor")),
        check_vma=False,
    )
```

```python
import functools

import jax
import jax.numpy as jnp
from jax import lax
from jax.experimental import pallas as pl
from jax.experimental.pallas import tpu as pltpu
from jax.sharding import PartitionSpec as P

ADAPTER_RANK = 16
ADAPTER_SCALE = 2.0
ROWS = 16
F32 = jnp.float32
BF16 = jnp.bfloat16
I32 = jnp.int32
NT = (((1,), (1,)), ((), ()))
VMEM_BYTES = 56 * 1024 * 1024
IN_VMEM = pl.BlockSpec(memory_space=pltpu.VMEM)
IN_SMEM = pl.BlockSpec(memory_space=pltpu.SMEM)
ANYWHERE = pl.BlockSpec(memory_space=pl.ANY)


def cost(flops, nbytes):
    return pl.CostEstimate(flops=int(flops) // 64, bytes_accessed=int(nbytes) // 64, transcendentals=0)


def params():
    return pltpu.CompilerParams(vmem_limit_bytes=VMEM_BYTES)


def pack_kernel(slot_ref, *refs):
    pieces, out_ref = refs[:-1], refs[-1]
    shape = (out_ref.shape[0], slot_ref.shape[1])
    pick = (lax.broadcasted_iota(I32, shape, 0) == slot_ref[...]).astype(F32).astype(BF16)
    rows = jnp.concatenate([piece[...] for piece in pieces], axis=0)
    out_ref[...] = jnp.dot(pick, rows, preferred_element_type=F32).astype(BF16)


def pack_rows(slot, pieces, slots):
    tokens, width = slot.shape[1], pieces[0].shape[1]
    tile = min(1024, width)
    column = lambda n: (0, n)
    return pl.pallas_call(
        pack_kernel,
        grid=(width // tile,),
        out_shape=jax.ShapeDtypeStruct((slots, width), BF16),
        in_specs=[pl.BlockSpec((1, tokens), lambda n: (0, 0))]
        + [pl.BlockSpec((piece.shape[0], tile), column) for piece in pieces],
        out_specs=pl.BlockSpec((slots, tile), column),
        compiler_params=params(),
        cost_estimate=cost(2 * tokens * slots * width, 2 * (tokens + slots) * width),
        name="pack_rows",
    )(slot, *pieces)


def masked_sum(projected, local, per_owner):
    total = jnp.zeros((ADAPTER_RANK, projected.shape[1]), F32)
    for j in range(per_owner):
        total = total + jnp.where(local == j, projected[j * ADAPTER_RANK : (j + 1) * ADAPTER_RANK], 0.0)
    return total


def repack_kernel(planes, per_owner, plane_ref, places_ref, local_ref, own_d_ref, other_d_ref, *refs):
    pieces = refs[: 2 * planes - 1]
    own_ref, other_ref, ranks_ref, rows, downs, sems, down_sems = refs[2 * planes - 1 :]
    here, below, above = pieces[0], pieces[1:planes], pieces[planes:]
    plane = plane_ref[0]

    def copy(source, d):
        return pltpu.make_async_copy(source, rows.at[d], sems.at[d])

    copy(here, 0).start()
    for d in range(1, planes):
        @pl.when(plane + d < planes)
        def _():
            copy(below[d - 1], d).start()

        @pl.when(plane + d >= planes)
        def _():
            copy(above[planes - d - 1], d).start()

    weights = [
        pltpu.make_async_copy(source, downs.at[i], down_sems.at[i]) for i, source in enumerate((own_d_ref, other_d_ref))
    ]
    for weight in weights:
        weight.start()
    tokens = here.shape[0]
    capacity = own_ref.shape[0] // planes
    row = lax.broadcasted_iota(I32, (2 * capacity, tokens), 0)
    for d in range(planes):
        copy(here, d).wait()
        pick = (row == places_ref[:, d * tokens : (d + 1) * tokens]).astype(F32).astype(BF16)
        packed = jnp.dot(pick, rows[d], preferred_element_type=F32).astype(BF16)
        own_ref[pl.ds(d * capacity, capacity), :] = packed[:capacity]
        other_ref[pl.ds(d * capacity, capacity), :] = packed[capacity:]
    for i, out_ref in enumerate((own_ref, other_ref)):
        weights[i].wait()
        projected = lax.dot_general(downs[i], out_ref[...], NT, preferred_element_type=F32)
        ranks_ref[i] = masked_sum(projected, local_ref[i : i + 1, :], per_owner)


def repack(plane, places, local, down_ts, here, below, above, capacity, per_owner):
    tokens, width = here.shape
    planes = len(below) + 1
    slots = planes * capacity
    rank_cols = down_ts[0].shape[0]
    return pl.pallas_call(
        functools.partial(repack_kernel, planes, per_owner),
        out_shape=[jax.ShapeDtypeStruct((slots, width), BF16)] * 2
        + [jax.ShapeDtypeStruct((2, ADAPTER_RANK, slots), F32)],
        in_specs=[IN_SMEM, IN_VMEM, IN_VMEM] + [ANYWHERE] * (2 * planes + 1),
        out_specs=[IN_VMEM] * 3,
        scratch_shapes=[
            pltpu.VMEM((planes, tokens, width), BF16),
            pltpu.VMEM((2, rank_cols, width), BF16),
            pltpu.SemaphoreType.DMA((planes,)),
            pltpu.SemaphoreType.DMA((2,)),
        ],
        compiler_params=params(),
        cost_estimate=cost(4 * slots * (tokens + rank_cols) * width, 2 * planes * (tokens + 2 * capacity) * width),
        name="repack",
    )(plane.reshape(1), places, local, *down_ts, here, *below, *above)


def ranks_kernel(per_owner, blocks, order_ref, local_ref, weight_ref, *refs):
    pieces, (out_ref, projected) = refs[:blocks], refs[blocks:]
    k = pl.program_id(0)
    rows = jnp.concatenate([piece[...] for piece in pieces], axis=0)
    part = lax.dot_general(weight_ref[...], rows, NT, preferred_element_type=F32)

    @pl.when(k == 0)
    def _():
        projected[...] = part

    @pl.when(k > 0)
    def _():
        projected[...] += part

    @pl.when(k == pl.num_programs(0) - 1)
    def _():
        out_ref[...] = masked_sum(projected, local_ref[...], per_owner)


def block_specs(blocks, capacity, tile):
    return [pl.BlockSpec((capacity, tile), lambda n, order, i=i: (order[i], n)) for i in range(blocks)]


def token_ranks(order, local, weight, slots, per_owner):
    blocks, width = order.shape[0], weight.shape[1]
    total = local.shape[1]
    rank_cols = weight.shape[0]
    tile = min(512, width)
    return pl.pallas_call(
        functools.partial(ranks_kernel, per_owner, blocks),
        out_shape=jax.ShapeDtypeStruct((ADAPTER_RANK, total), F32),
        grid_spec=pltpu.PrefetchScalarGridSpec(
            num_scalar_prefetch=1,
            grid=(width // tile,),
            in_specs=[
                pl.BlockSpec((1, total), lambda n, order: (0, 0)),
                pl.BlockSpec((rank_cols, tile), lambda n, order: (0, n)),
            ]
            + block_specs(blocks, total // blocks, tile),
            out_specs=pl.BlockSpec((ADAPTER_RANK, total), lambda n, order: (0, 0)),
            scratch_shapes=[pltpu.VMEM((rank_cols, total), F32)],
        ),
        compiler_params=params(),
        cost_estimate=cost(2 * total * width * rank_cols, 2 * width * (total + rank_cols)),
        name="token_ranks",
    )(order, local, weight, *[slots] * blocks)


def load_rows(names, place_ref, pieces, rows, sems):
    me = place_ref[0]
    copies = []
    for (first, ks), piece in zip(names, pieces):
        blocks = pl.ds(first, piece.shape[1])
        for j, k in enumerate(ks):
            copies.append(pltpu.make_async_copy(piece.at[j], rows.at[blocks, me ^ k], sems.at[len(copies)]))
            copies[-1].start()
    for copy in copies:
        copy.wait()


def frozen_kernel(names, place_ref, own_w_ref, other_w_ref, *refs):
    pieces, (out_ref, rows, sems) = refs[:-3], refs[-3:]
    blocks, tensors, sub, _ = rows.shape
    tokens = tensors * sub
    depth = own_w_ref.shape[1]

    @pl.when(pl.program_id(0) == 0)
    def _():
        load_rows(names, place_ref, pieces, rows, sems)

    for b in range(blocks):
        x = rows[b].reshape(tokens, 2 * depth)
        product = lax.dot_general(x[:, :depth], own_w_ref[...], NT, preferred_element_type=F32)
        product += lax.dot_general(x[:, depth:], other_w_ref[...], NT, preferred_element_type=F32)
        out_ref[pl.ds(b * tokens, tokens), :] = product


def frozen_part(tensor, weights, names, pieces):
    _, blocks, sub, cols = pieces[0].shape
    blocks, tensors = 2 * blocks, sum(len(ks) for _, ks in names) // 2
    rows = blocks * sub * tensors
    width, depth = weights[0].shape
    tile = min(512, width)
    return pl.pallas_call(
        functools.partial(frozen_kernel, names),
        grid=(width // tile,),
        out_shape=jax.ShapeDtypeStruct((rows, width), F32),
        in_specs=[IN_SMEM] + [pl.BlockSpec((tile, depth), lambda n: (n, 0))] * 2 + [ANYWHERE] * len(pieces),
        out_specs=pl.BlockSpec((rows, tile), lambda n: (0, n)),
        scratch_shapes=[pltpu.VMEM((blocks, tensors, sub, cols), BF16), pltpu.SemaphoreType.DMA((2 * tensors,))],
        compiler_params=params(),
        cost_estimate=cost(2 * rows * width * cols, 4 * rows * width + 4 * width * depth),
        name="frozen_part",
    )(tensor.reshape(1), *weights, *pieces)


def spread_rows(wide, first, local, ranks, per_owner):
    for j in range(per_owner):
        wide[pl.ds(first + j * ADAPTER_RANK, ADAPTER_RANK), :] = jnp.where(local == j, ranks, 0.0).astype(BF16)


def term_kernel(per_owner, frozen_ref, places_ref, *refs):
    ranks, downs, out_refs, (wide, flat) = refs[:2], refs[2:4], refs[4:-2], refs[-2:]
    rank_cols = downs[0].shape[0]

    @pl.when(pl.program_id(0) == 0)
    def _():
        for i in range(2):
            slot, local = places_ref[i : i + 1, :], places_ref[i + 2 : i + 3, :]
            pick = lax.broadcasted_iota(I32, (ranks[i].shape[1], slot.shape[1]), 0) == slot
            in_order = jnp.dot(ranks[i][...], pick.astype(F32).astype(BF16), preferred_element_type=F32)
            spread_rows(wide, i * rank_cols, local, in_order, per_owner)
        flat[...] = wide[...].T

    total = frozen_ref[...]
    total += jnp.dot(flat[:, :rank_cols], downs[0][...], preferred_element_type=F32)
    total += jnp.dot(flat[:, rank_cols:], downs[1][...], preferred_element_type=F32)
    rows = total.shape[0] // len(out_refs)
    for i, out_ref in enumerate(out_refs):
        out_ref[...] = total[i * rows : (i + 1) * rows].astype(out_ref.dtype)


def add_term(frozen, first, rows, places, ranks, downs, per_owner, types):
    width = frozen.shape[1]
    rank_cols = downs[0].shape[0]
    tile = min(512, width)
    column = lambda n: (0, n)
    each = rows // len(types)
    return pl.pallas_call(
        functools.partial(term_kernel, per_owner),
        grid=(width // tile,),
        out_shape=[jax.ShapeDtypeStruct((each, width), kind) for kind in types],
        in_specs=[
            pl.BlockSpec((rows, tile), lambda n: (first, n)),
            pl.BlockSpec((places.shape[0], rows), lambda n: (0, first)),
        ]
        + [pl.BlockSpec(x.shape, lambda n: (0, 0)) for x in ranks]
        + [pl.BlockSpec((rank_cols, tile), column)] * 2,
        out_specs=[pl.BlockSpec((each, tile), column)] * len(types),
        scratch_shapes=[pltpu.VMEM((2 * rank_cols, rows), BF16), pltpu.VMEM((rows, 2 * rank_cols), BF16)],
        compiler_params=params(),
        cost_estimate=cost(4 * rows * width * rank_cols, 6 * rows * width + 4 * rank_cols * width),
        name="add_term",
    )(frozen, places, *ranks, *downs)


def gradients_kernel(per_owner, blocks, order_ref, local_ref, grad_ranks_ref, up_ranks_ref, own_ref, other_ref, *refs):
    grad, (down_ref, up_ref, flat_grad, wide_up) = refs[:blocks], refs[blocks:]

    @pl.when(pl.program_id(0) == 0)
    def _():
        local = local_ref[...]
        spread_rows(wide_up, 0, local, grad_ranks_ref[...].astype(F32), per_owner)
        flat_grad[...] = wide_up[...].T
        spread_rows(wide_up, 0, local, up_ranks_ref[...].astype(F32), per_owner)

    rows = jnp.concatenate([own_ref[...], other_ref[...]], axis=0)
    down_ref[...] = lax.dot_general(rows, flat_grad[...], (((0,), (0,)), ((), ())), preferred_element_type=F32)
    rows = jnp.concatenate([piece[...] for piece in grad], axis=0)
    up_ref[...] = jnp.dot(wide_up[...], rows, preferred_element_type=F32)


def adapter_gradients(order, local, grad_ranks, up_ranks, attn, grad, per_owner):
    total, width = grad.shape
    blocks = order.shape[0]
    rank_cols = per_owner * ADAPTER_RANK
    tile = min(256, width)
    whole = lambda n, order: (0, 0)
    column = lambda n, order: (0, n)
    return pl.pallas_call(
        functools.partial(gradients_kernel, per_owner, blocks),
        out_shape=(
            jax.ShapeDtypeStruct((width, rank_cols), F32),
            jax.ShapeDtypeStruct((rank_cols, width), F32),
        ),
        grid_spec=pltpu.PrefetchScalarGridSpec(
            num_scalar_prefetch=1,
            grid=(width // tile,),
            in_specs=[pl.BlockSpec((1, total), whole)]
            + [pl.BlockSpec((ADAPTER_RANK, total), whole)] * 2
            + [pl.BlockSpec((total // 2, tile), column)] * 2
            + block_specs(blocks, total // blocks, tile),
            out_specs=(
                pl.BlockSpec((tile, rank_cols), lambda n, order: (n, 0)),
                pl.BlockSpec((rank_cols, tile), column),
            ),
            scratch_shapes=[pltpu.VMEM((total, rank_cols), BF16), pltpu.VMEM((rank_cols, total), BF16)],
        ),
        compiler_params=params(),
        cost_estimate=cost(4 * total * width * rank_cols, 4 * total * width + 8 * rank_cols * width),
        name="adapter_gradients",
    )(order, local, grad_ranks, up_ranks, *attn, *[grad] * blocks)


def per_device(attn, grad, ids, weight, down, up):
    owners = lax.axis_size("adapter")
    tensors = lax.axis_size("tensor")
    planes = owners // 2
    me = lax.axis_index("adapter")
    plane, core = me // 2, me % 2
    tensor = lax.axis_index("tensor")
    tokens, width = attn.shape
    sub = grad.shape[0]
    out_cols = weight.shape[1]
    rank_cols = down.shape[1]
    per_owner = rank_cols // ADAPTER_RANK
    capacity = -(-5 * tokens // (2 * owners) // ROWS) * ROWS
    slot_count = owners * capacity

    def shift(x, by):
        pairs = [(2 * z + c, 2 * ((z + by) % planes) + c) for z in range(planes) for c in range(2)]
        return lax.ppermute(x, "adapter", pairs)

    def up_line(x, distance):
        pairs = [(2 * z + c, 2 * z + 2 + c) for z in range(planes - distance) for c in range(2)]
        return lax.ppermute(x, "adapter", pairs)

    def down_line(x, distance):
        pairs = [(2 * z + c, 2 * z - 2 + c) for z in range(distance, planes) for c in range(2)]
        return lax.ppermute(x, "adapter", pairs)

    def attn_line(x, d, way):
        planes_on = range(d - 1, planes - 1) if way == 1 else range(1, planes - d + 1)
        return lax.ppermute(x, "adapter", [(2 * z + c, 2 * (z + way) + c) for z in planes_on for c in range(2)])

    def swap(x):
        return lax.ppermute(x, "adapter", [(a, a ^ 1) for a in range(owners)])

    def flip(x, k):
        return lax.ppermute(x, "tensor", [(t, t ^ k) for t in range(tensors)])

    def after(x, *others):
        return lax.optimization_barrier((x, *others))[0]

    def tensor_cols(k):
        return lax.dynamic_slice_in_dim(grad, (tensor ^ k) * width, width, 1)

    tensor_parts = [tensor_cols(k) for k in range(tensors)]
    grad_rows = tensor_parts[:1] + [flip(tensor_parts[k], k) for k in range(1, tensors)]
    grad_again, ids_again = after((grad, ids), *tensor_parts)

    def plane_cols(offset):
        p = (plane + offset) % planes
        parts = [
            lax.dynamic_slice_in_dim(grad_again, (2 * p + c) * out_cols, out_cols, 1) for c in (core, 1 - core)
        ]
        return jnp.concatenate(parts, axis=1)

    half = planes // 2
    order = [d for s in range(1, half) for d in (s, planes - s)] + [half, 0]
    plane_parts = [plane_cols(d) for d in range(planes)]
    part = {0: plane_parts[0]}
    for d in range(1, planes):
        part[planes - d] = shift(plane_parts[d], d)
    ids_again = after(ids_again, *plane_parts, *grad_rows[1:])

    all_ids = lax.all_to_all(jnp.broadcast_to(ids_again, (owners, tokens)), "adapter", 0, 0, tiled=True)

    def placing(block_ids):
        owner = block_ids // per_owner
        earlier = jnp.arange(tokens)[:, None] > jnp.arange(tokens)[None, :]
        same = owner[..., :, None] == owner[..., None, :]
        place = jnp.sum((same & earlier).astype(I32), axis=-1)
        return owner, place

    owner, place = placing(ids)
    slot = owner * capacity + place
    slot_here = jnp.concatenate(
        [lax.dynamic_slice_in_dim(slot, (tensor ^ k) * sub, sub, 0) for k in range(tensors)]
    )
    down_t = down.T
    grad_packed = pack_rows(slot_here.reshape(1, -1), after(grad_rows, down_t), slot_count)

    def to_owners(x):
        x = x.reshape(owners, capacity, width)
        return lax.all_to_all(x, "adapter", 0, 0, tiled=True).reshape(slot_count, width)

    grad_packed = after(grad_packed, *(part[d] for d in range(1, planes)))
    grad_slots = to_owners(grad_packed)

    halves = [jnp.stack([part[d] for d in order[i * half : (i + 1) * half]], axis=0) for i in range(2)]
    bits = [1 << i for i in range(tensors.bit_length() - 1)]
    plane_rows = [[([0], x[None])] for x in halves]
    for step in zip(bits, reversed(bits)):
        for rows, bit in zip(plane_rows, step):
            sent = jnp.concatenate([x for _, x in rows], axis=0) if len(rows) > 1 else rows[0][1]
            rows.append(([k ^ bit for ks, _ in rows for k in ks], flip(sent, bit)))
    first_rows = [rows[1][1] for rows in plane_rows]
    row_names = [(i * half, ks) for i, rows in enumerate(plane_rows) for ks, _ in rows]
    plane_rows = [x for rows in plane_rows for _, x in rows]
    all_ids = after(all_ids, *first_rows)
    other_weight = swap(weight)
    other_down_t = swap(down_t)

    ahead = [2 * ((plane + jnp.arange(planes)) % planes) + c for c in (core, 1 - core)]
    slot_order = jnp.concatenate(ahead)
    near_ids = all_ids[slot_order]
    near_owner, near_place = placing(near_ids)

    def labels(owner, blocks):
        mine = (near_owner[blocks] == owner)[:, None, :]
        mine &= near_place[blocks][:, None, :] == jnp.arange(capacity, dtype=I32)[:, None]
        from_first = near_ids[blocks][:, None, :] - owner * per_owner
        return (jnp.sum(jnp.where(mine, from_first + 1, 0), axis=-1) - 1).reshape(1, -1)

    parity = slice(0, planes)
    here, there = labels(me, parity), labels(me, slice(planes, owners))
    local = jnp.concatenate([here, there], axis=1)
    parity_local = jnp.concatenate([here, labels(me ^ 1, parity)], axis=0)

    parity_ids, parity_owner, parity_place = near_ids[parity], near_owner[parity], near_place[parity]
    attn_places = jnp.where(parity_owner == me, parity_place, -1)
    attn_places = jnp.where(parity_owner == (me ^ 1), parity_place + capacity, attn_places).reshape(1, -1)
    base = capacity * jnp.arange(planes, dtype=I32)[:, None]
    places = jnp.stack(
        [
            jnp.where(parity_owner == me, parity_place + base, -1),
            jnp.where(parity_owner == (me ^ 1), parity_place + base + planes * capacity, -1),
            parity_ids - me * per_owner,
            parity_ids - (me ^ 1) * per_owner,
        ]
    )
    places = jnp.concatenate([places[:, d : d + 1] for d in order], axis=1).reshape(4, -1)

    first_weight = after(weight, places, local, parity_local, attn_places, slot_order, other_down_t)
    attn_start = after(attn, *first_rows)
    going_down, going_up = attn_line(attn_start, 1, -1), attn_line(attn_start, 1, 1)
    frozen = frozen_part(tensor, (first_weight, other_weight), row_names, plane_rows)
    grad_slots = after(grad_slots, frozen)
    part_grads = token_ranks(slot_order, local, up, grad_slots, per_owner)
    low_grads = sum([flip(part_grads, k) for k in range(1, tensors)], part_grads)
    grad_low = (ADAPTER_SCALE * low_grads).astype(BF16)
    ranks = (grad_low, swap(grad_low))
    downs = (down_t, other_down_t)

    def with_term(i, types):
        return add_term(frozen, i, half * tokens, places, ranks, downs, per_owner, types)

    pairs = with_term(0, [BF16] * planes)
    below, above = [going_down], [going_up]
    for d in range(2, planes):
        if d == 2:
            going_down, going_up = after((going_down, going_up), *pairs)
        going_down, going_up = attn_line(going_down, d, -1), attn_line(going_up, d, 1)
        below.append(going_down)
        above.append(going_up)
    pairs += with_term(1, [BF16] * (planes - 2) + [F32] * 2)
    sums = {d: pairs[2 * i : 2 * i + 2] for i, d in enumerate(order)}
    going_up, going_down = [None, None], [None, None]
    for d in range(planes - 1, 0, -1):
        for i in range(2):
            up_sum, down_sum = sums[d][i], sums[planes - d][i]
            if going_up[i] is not None:
                up_sum = (up_sum.astype(F32) + going_up[i].astype(F32)).astype(BF16)
                down_sum = (down_sum.astype(F32) + going_down[i].astype(F32)).astype(BF16)
            if i == 0:
                last_sums = (up_sum, down_sum)
            going_up[i], going_down[i] = up_line(up_sum, d), down_line(down_sum, d)
    below[-1], above[-1] = after((below[-1], above[-1]), *last_sums)
    attn_own, attn_other, parity_inputs = repack(
        plane, attn_places, parity_local, downs, attn, below, above, capacity, per_owner
    )
    attn_slots = [attn_own, swap(attn_other)]
    low_inputs = sum([flip(parity_inputs, k) for k in range(1, tensors)], parity_inputs)
    up_scaled = (ADAPTER_SCALE * low_inputs).astype(BF16)
    up_scaled = jnp.concatenate([up_scaled[0], swap(up_scaled[1])], axis=1)
    down_grad, up_grad = adapter_gradients(slot_order, local, grad_low, up_scaled, attn_slots, grad_slots, per_owner)
    going_up, going_down = after((going_up, going_down), down_grad)
    total = [x + up_sum.astype(F32) + down_sum.astype(F32) for x, up_sum, down_sum in zip(sums[0], going_up, going_down)]
    attention_output_gradient = jnp.concatenate(total, axis=0).astype(BF16)
    return attention_output_gradient, down_grad, up_grad


def solution(mesh):
    placed = (
        P("adapter", "tensor"),
        P(("adapter", "tensor"), None),
        P("adapter"),
        P("tensor", "adapter"),
        P("tensor", "adapter"),
        P("adapter", "tensor"),
    )
    return jax.shard_map(
        per_device,
        mesh=mesh,
        in_specs=placed,
        out_specs=(P("adapter", "tensor"), P("tensor", "adapter"), P("adapter", "tensor")),
        check_vma=False,
    )
```

```python
import functools

import jax
import jax.numpy as jnp
from jax import lax
from jax.experimental import pallas as pl
from jax.experimental.pallas import tpu as pltpu
from jax.sharding import PartitionSpec as P

ADAPTER_RANK = 16
ADAPTER_SCALE = 2.0
ROWS = 16
F32 = jnp.float32
BF16 = jnp.bfloat16
I32 = jnp.int32
NT = (((1,), (1,)), ((), ()))
VMEM_BYTES = 56 * 1024 * 1024
IN_VMEM = pl.BlockSpec(memory_space=pltpu.VMEM)
IN_SMEM = pl.BlockSpec(memory_space=pltpu.SMEM)
ANYWHERE = pl.BlockSpec(memory_space=pl.ANY)


def cost(flops, nbytes):
    return pl.CostEstimate(flops=int(flops) // 64, bytes_accessed=int(nbytes) // 64, transcendentals=0)


def params():
    return pltpu.CompilerParams(vmem_limit_bytes=VMEM_BYTES)


def pack_kernel(slot_ref, *refs):
    pieces, out_ref = refs[:-1], refs[-1]
    shape = (out_ref.shape[0], slot_ref.shape[1])
    pick = (lax.broadcasted_iota(I32, shape, 0) == slot_ref[...]).astype(F32).astype(BF16)
    rows = jnp.concatenate([piece[...] for piece in pieces], axis=0)
    out_ref[...] = jnp.dot(pick, rows, preferred_element_type=F32).astype(BF16)


def pack_rows(slot, pieces, slots):
    tokens, width = slot.shape[1], pieces[0].shape[1]
    tile = min(1024, width)
    column = lambda n: (0, n)
    return pl.pallas_call(
        pack_kernel,
        grid=(width // tile,),
        out_shape=jax.ShapeDtypeStruct((slots, width), BF16),
        in_specs=[pl.BlockSpec((1, tokens), lambda n: (0, 0))]
        + [pl.BlockSpec((piece.shape[0], tile), column) for piece in pieces],
        out_specs=pl.BlockSpec((slots, tile), column),
        compiler_params=params(),
        cost_estimate=cost(2 * tokens * slots * width, 2 * (tokens + slots) * width),
        name="pack_rows",
    )(slot, *pieces)


def masked_sum(projected, local, per_owner):
    total = jnp.zeros((ADAPTER_RANK, projected.shape[1]), F32)
    for j in range(per_owner):
        total = total + jnp.where(local == j, projected[j * ADAPTER_RANK : (j + 1) * ADAPTER_RANK], 0.0)
    return total


def repack_kernel(planes, per_owner, plane_ref, places_ref, local_ref, own_d_ref, other_d_ref, *refs):
    pieces = refs[: 2 * planes - 1]
    own_ref, other_ref, ranks_ref, rows, downs, sems, down_sems = refs[2 * planes - 1 :]
    here, below, above = pieces[0], pieces[1:planes], pieces[planes:]
    plane = plane_ref[0]

    def copy(source, d):
        return pltpu.make_async_copy(source, rows.at[d], sems.at[d])

    copy(here, 0).start()
    for d in range(1, planes):
        @pl.when(plane + d < planes)
        def _():
            copy(below[d - 1], d).start()

        @pl.when(plane + d >= planes)
        def _():
            copy(above[planes - d - 1], d).start()

    weights = [
        pltpu.make_async_copy(source, downs.at[i], down_sems.at[i]) for i, source in enumerate((own_d_ref, other_d_ref))
    ]
    for weight in weights:
        weight.start()
    tokens = here.shape[0]
    capacity = own_ref.shape[0] // planes
    row = lax.broadcasted_iota(I32, (2 * capacity, tokens), 0)
    for d in range(planes):
        copy(here, d).wait()
        pick = (row == places_ref[:, d * tokens : (d + 1) * tokens]).astype(F32).astype(BF16)
        packed = jnp.dot(pick, rows[d], preferred_element_type=F32).astype(BF16)
        own_ref[pl.ds(d * capacity, capacity), :] = packed[:capacity]
        other_ref[pl.ds(d * capacity, capacity), :] = packed[capacity:]
    for i, out_ref in enumerate((own_ref, other_ref)):
        weights[i].wait()
        projected = lax.dot_general(downs[i], out_ref[...], NT, preferred_element_type=F32)
        ranks_ref[i] = masked_sum(projected, local_ref[i : i + 1, :], per_owner)


def repack(plane, places, local, down_ts, here, below, above, capacity, per_owner):
    tokens, width = here.shape
    planes = len(below) + 1
    slots = planes * capacity
    rank_cols = down_ts[0].shape[0]
    return pl.pallas_call(
        functools.partial(repack_kernel, planes, per_owner),
        out_shape=[jax.ShapeDtypeStruct((slots, width), BF16)] * 2
        + [jax.ShapeDtypeStruct((2, ADAPTER_RANK, slots), F32)],
        in_specs=[IN_SMEM, IN_VMEM, IN_VMEM] + [ANYWHERE] * (2 * planes + 1),
        out_specs=[IN_VMEM] * 3,
        scratch_shapes=[
            pltpu.VMEM((planes, tokens, width), BF16),
            pltpu.VMEM((2, rank_cols, width), BF16),
            pltpu.SemaphoreType.DMA((planes,)),
            pltpu.SemaphoreType.DMA((2,)),
        ],
        compiler_params=params(),
        cost_estimate=cost(4 * slots * (tokens + rank_cols) * width, 2 * planes * (tokens + 2 * capacity) * width),
        name="repack",
    )(plane.reshape(1), places, local, *down_ts, here, *below, *above)


def ranks_kernel(per_owner, blocks, order_ref, local_ref, weight_ref, *refs):
    pieces, (out_ref, projected) = refs[:blocks], refs[blocks:]
    k = pl.program_id(0)
    rows = jnp.concatenate([piece[...] for piece in pieces], axis=0)
    part = lax.dot_general(weight_ref[...], rows, NT, preferred_element_type=F32)

    @pl.when(k == 0)
    def _():
        projected[...] = part

    @pl.when(k > 0)
    def _():
        projected[...] += part

    @pl.when(k == pl.num_programs(0) - 1)
    def _():
        out_ref[...] = masked_sum(projected, local_ref[...], per_owner)


def block_specs(blocks, capacity, tile):
    return [pl.BlockSpec((capacity, tile), lambda n, order, i=i: (order[i], n)) for i in range(blocks)]


def token_ranks(order, local, weight, slots, per_owner):
    blocks, width = order.shape[0], weight.shape[1]
    total = local.shape[1]
    rank_cols = weight.shape[0]
    tile = min(1024, width)
    return pl.pallas_call(
        functools.partial(ranks_kernel, per_owner, blocks),
        out_shape=jax.ShapeDtypeStruct((ADAPTER_RANK, total), F32),
        grid_spec=pltpu.PrefetchScalarGridSpec(
            num_scalar_prefetch=1,
            grid=(width // tile,),
            in_specs=[
                pl.BlockSpec((1, total), lambda n, order: (0, 0)),
                pl.BlockSpec((rank_cols, tile), lambda n, order: (0, n)),
            ]
            + block_specs(blocks, total // blocks, tile),
            out_specs=pl.BlockSpec((ADAPTER_RANK, total), lambda n, order: (0, 0)),
            scratch_shapes=[pltpu.VMEM((rank_cols, total), F32)],
        ),
        compiler_params=params(),
        cost_estimate=cost(2 * total * width * rank_cols, 2 * width * (total + rank_cols)),
        name="token_ranks",
    )(order, local, weight, *[slots] * blocks)


def load_rows(names, place_ref, pieces, rows, sems):
    me = place_ref[0]
    copies = []
    for (first, ks), piece in zip(names, pieces):
        blocks = pl.ds(first, piece.shape[1])
        for j, k in enumerate(ks):
            copies.append(pltpu.make_async_copy(piece.at[j], rows.at[blocks, me ^ k], sems.at[len(copies)]))
            copies[-1].start()
    for copy in copies:
        copy.wait()


def frozen_kernel(names, place_ref, own_w_ref, other_w_ref, *refs):
    pieces, (out_ref, rows, sems) = refs[:-3], refs[-3:]
    blocks, tensors, sub, _ = rows.shape
    tokens = tensors * sub
    depth = own_w_ref.shape[1]

    @pl.when(pl.program_id(0) == 0)
    def _():
        load_rows(names, place_ref, pieces, rows, sems)

    for b in range(blocks):
        x = rows[b].reshape(tokens, 2 * depth)
        product = lax.dot_general(x[:, :depth], own_w_ref[...], NT, preferred_element_type=F32)
        product += lax.dot_general(x[:, depth:], other_w_ref[...], NT, preferred_element_type=F32)
        out_ref[pl.ds(b * tokens, tokens), :] = product


def frozen_part(tensor, weights, names, pieces):
    _, blocks, sub, cols = pieces[0].shape
    blocks, tensors = 2 * blocks, sum(len(ks) for _, ks in names) // 2
    rows = blocks * sub * tensors
    width, depth = weights[0].shape
    tile = min(512, width)
    return pl.pallas_call(
        functools.partial(frozen_kernel, names),
        grid=(width // tile,),
        out_shape=jax.ShapeDtypeStruct((rows, width), F32),
        in_specs=[IN_SMEM] + [pl.BlockSpec((tile, depth), lambda n: (n, 0))] * 2 + [ANYWHERE] * len(pieces),
        out_specs=pl.BlockSpec((rows, tile), lambda n: (0, n)),
        scratch_shapes=[pltpu.VMEM((blocks, tensors, sub, cols), BF16), pltpu.SemaphoreType.DMA((2 * tensors,))],
        compiler_params=params(),
        cost_estimate=cost(2 * rows * width * cols, 4 * rows * width + 4 * width * depth),
        name="frozen_part",
    )(tensor.reshape(1), *weights, *pieces)


def spread_rows(wide, first, local, ranks, per_owner):
    for j in range(per_owner):
        wide[pl.ds(first + j * ADAPTER_RANK, ADAPTER_RANK), :] = jnp.where(local == j, ranks, 0.0).astype(BF16)


def term_kernel(per_owner, frozen_ref, places_ref, *refs):
    ranks, downs, out_refs, (wide, flat) = refs[:2], refs[2:4], refs[4:-2], refs[-2:]
    rank_cols = downs[0].shape[0]

    @pl.when(pl.program_id(0) == 0)
    def _():
        for i in range(2):
            slot, local = places_ref[i : i + 1, :], places_ref[i + 2 : i + 3, :]
            pick = lax.broadcasted_iota(I32, (ranks[i].shape[1], slot.shape[1]), 0) == slot
            in_order = jnp.dot(ranks[i][...], pick.astype(F32).astype(BF16), preferred_element_type=F32)
            spread_rows(wide, i * rank_cols, local, in_order, per_owner)
        flat[...] = wide[...].T

    total = frozen_ref[...]
    total += jnp.dot(flat[:, :rank_cols], downs[0][...], preferred_element_type=F32)
    total += jnp.dot(flat[:, rank_cols:], downs[1][...], preferred_element_type=F32)
    rows = total.shape[0] // len(out_refs)
    for i, out_ref in enumerate(out_refs):
        out_ref[...] = total[i * rows : (i + 1) * rows].astype(out_ref.dtype)


def add_term(frozen, first, rows, places, ranks, downs, per_owner, types):
    width = frozen.shape[1]
    rank_cols = downs[0].shape[0]
    tile = min(1024, width)
    column = lambda n: (0, n)
    each = rows // len(types)
    return pl.pallas_call(
        functools.partial(term_kernel, per_owner),
        grid=(width // tile,),
        out_shape=[jax.ShapeDtypeStruct((each, width), kind) for kind in types],
        in_specs=[
            pl.BlockSpec((rows, tile), lambda n: (first, n)),
            pl.BlockSpec((places.shape[0], rows), lambda n: (0, first)),
        ]
        + [pl.BlockSpec(x.shape, lambda n: (0, 0)) for x in ranks]
        + [pl.BlockSpec((rank_cols, tile), column)] * 2,
        out_specs=[pl.BlockSpec((each, tile), column)] * len(types),
        scratch_shapes=[pltpu.VMEM((2 * rank_cols, rows), BF16), pltpu.VMEM((rows, 2 * rank_cols), BF16)],
        compiler_params=params(),
        cost_estimate=cost(4 * rows * width * rank_cols, 6 * rows * width + 4 * rank_cols * width),
        name="add_term",
    )(frozen, places, *ranks, *downs)


def gradients_kernel(per_owner, blocks, order_ref, local_ref, grad_ranks_ref, up_ranks_ref, own_ref, other_ref, *refs):
    grad, (down_ref, up_ref, flat_grad, wide_up) = refs[:blocks], refs[blocks:]

    @pl.when(pl.program_id(0) == 0)
    def _():
        local = local_ref[...]
        spread_rows(wide_up, 0, local, grad_ranks_ref[...].astype(F32), per_owner)
        flat_grad[...] = wide_up[...].T
        spread_rows(wide_up, 0, local, up_ranks_ref[...].astype(F32), per_owner)

    rows = jnp.concatenate([own_ref[...], other_ref[...]], axis=0)
    down_ref[...] = lax.dot_general(rows, flat_grad[...], (((0,), (0,)), ((), ())), preferred_element_type=F32)
    rows = jnp.concatenate([piece[...] for piece in grad], axis=0)
    up_ref[...] = jnp.dot(wide_up[...], rows, preferred_element_type=F32)


def adapter_gradients(order, local, grad_ranks, up_ranks, attn, grad, per_owner):
    total, width = grad.shape
    blocks = order.shape[0]
    rank_cols = per_owner * ADAPTER_RANK
    tile = min(512, width)
    whole = lambda n, order: (0, 0)
    column = lambda n, order: (0, n)
    return pl.pallas_call(
        functools.partial(gradients_kernel, per_owner, blocks),
        out_shape=(
            jax.ShapeDtypeStruct((width, rank_cols), F32),
            jax.ShapeDtypeStruct((rank_cols, width), F32),
        ),
        grid_spec=pltpu.PrefetchScalarGridSpec(
            num_scalar_prefetch=1,
            grid=(width // tile,),
            in_specs=[pl.BlockSpec((1, total), whole)]
            + [pl.BlockSpec((ADAPTER_RANK, total), whole)] * 2
            + [pl.BlockSpec((total // 2, tile), column)] * 2
            + block_specs(blocks, total // blocks, tile),
            out_specs=(
                pl.BlockSpec((tile, rank_cols), lambda n, order: (n, 0)),
                pl.BlockSpec((rank_cols, tile), column),
            ),
            scratch_shapes=[pltpu.VMEM((total, rank_cols), BF16), pltpu.VMEM((rank_cols, total), BF16)],
        ),
        compiler_params=params(),
        cost_estimate=cost(4 * total * width * rank_cols, 4 * total * width + 8 * rank_cols * width),
        name="adapter_gradients",
    )(order, local, grad_ranks, up_ranks, *attn, *[grad] * blocks)


def per_device(attn, grad, ids, weight, down, up):
    owners = lax.axis_size("adapter")
    tensors = lax.axis_size("tensor")
    planes = owners // 2
    me = lax.axis_index("adapter")
    plane, core = me // 2, me % 2
    tensor = lax.axis_index("tensor")
    tokens, width = attn.shape
    sub = grad.shape[0]
    out_cols = weight.shape[1]
    rank_cols = down.shape[1]
    per_owner = rank_cols // ADAPTER_RANK
    capacity = -(-5 * tokens // (2 * owners) // ROWS) * ROWS
    slot_count = owners * capacity

    def shift(x, by):
        pairs = [(2 * z + c, 2 * ((z + by) % planes) + c) for z in range(planes) for c in range(2)]
        return lax.ppermute(x, "adapter", pairs)

    def up_line(x, distance):
        pairs = [(2 * z + c, 2 * z + 2 + c) for z in range(planes - distance) for c in range(2)]
        return lax.ppermute(x, "adapter", pairs)

    def down_line(x, distance):
        pairs = [(2 * z + c, 2 * z - 2 + c) for z in range(distance, planes) for c in range(2)]
        return lax.ppermute(x, "adapter", pairs)

    def attn_line(x, d, way):
        planes_on = range(d - 1, planes - 1) if way == 1 else range(1, planes - d + 1)
        return lax.ppermute(x, "adapter", [(2 * z + c, 2 * (z + way) + c) for z in planes_on for c in range(2)])

    def swap(x):
        return lax.ppermute(x, "adapter", [(a, a ^ 1) for a in range(owners)])

    def flip(x, k):
        return lax.ppermute(x, "tensor", [(t, t ^ k) for t in range(tensors)])

    def after(x, *others):
        return lax.optimization_barrier((x, *others))[0]

    def tensor_cols(k):
        return lax.dynamic_slice_in_dim(grad, (tensor ^ k) * width, width, 1)

    tensor_parts = [tensor_cols(k) for k in range(tensors)]
    grad_rows = tensor_parts[:1] + [flip(tensor_parts[k], k) for k in range(1, tensors)]
    grad_again, ids_again = after((grad, ids), *tensor_parts)

    def plane_cols(offset):
        p = (plane + offset) % planes
        parts = [
            lax.dynamic_slice_in_dim(grad_again, (2 * p + c) * out_cols, out_cols, 1) for c in (core, 1 - core)
        ]
        return jnp.concatenate(parts, axis=1)

    half = planes // 2
    order = [d for s in range(1, half) for d in (s, planes - s)] + [half, 0]
    plane_parts = [plane_cols(d) for d in range(planes)]
    part = {0: plane_parts[0]}
    for d in range(1, planes):
        part[planes - d] = shift(plane_parts[d], d)
    ids_again = after(ids_again, *plane_parts, *grad_rows[1:])

    all_ids = lax.all_to_all(jnp.broadcast_to(ids_again, (owners, tokens)), "adapter", 0, 0, tiled=True)

    def placing(block_ids):
        owner = block_ids // per_owner
        earlier = jnp.arange(tokens)[:, None] > jnp.arange(tokens)[None, :]
        same = owner[..., :, None] == owner[..., None, :]
        place = jnp.sum((same & earlier).astype(I32), axis=-1)
        return owner, place

    owner, place = placing(ids)
    slot = owner * capacity + place
    slot_here = jnp.concatenate(
        [lax.dynamic_slice_in_dim(slot, (tensor ^ k) * sub, sub, 0) for k in range(tensors)]
    )
    down_t = down.T
    grad_packed = pack_rows(slot_here.reshape(1, -1), after(grad_rows, down_t), slot_count)

    def to_owners(x):
        x = x.reshape(owners, capacity, width)
        return lax.all_to_all(x, "adapter", 0, 0, tiled=True).reshape(slot_count, width)

    grad_packed = after(grad_packed, part[1], part[planes - 1])
    grad_slots = to_owners(grad_packed)

    halves = [jnp.stack([part[d] for d in order[i * half : (i + 1) * half]], axis=0) for i in range(2)]
    bits = [1 << i for i in range(tensors.bit_length() - 1)]
    plane_rows = [[([0], x[None])] for x in halves]
    for step in zip(bits, reversed(bits)):
        for rows, bit in zip(plane_rows, step):
            sent = jnp.concatenate([x for _, x in rows], axis=0) if len(rows) > 1 else rows[0][1]
            rows.append(([k ^ bit for ks, _ in rows for k in ks], flip(sent, bit)))
    first_rows = [rows[1][1] for rows in plane_rows]
    row_names = [(i * half, ks) for i, rows in enumerate(plane_rows) for ks, _ in rows]
    plane_rows = [x for rows in plane_rows for _, x in rows]
    all_ids = after(all_ids, *first_rows)
    other_weight = swap(weight)
    other_down_t = swap(down_t)

    ahead = [2 * ((plane + jnp.arange(planes)) % planes) + c for c in (core, 1 - core)]
    slot_order = jnp.concatenate(ahead)
    near_ids = all_ids[slot_order]
    near_owner, near_place = placing(near_ids)

    def labels(owner, blocks):
        mine = (near_owner[blocks] == owner)[:, None, :]
        mine &= near_place[blocks][:, None, :] == jnp.arange(capacity, dtype=I32)[:, None]
        from_first = near_ids[blocks][:, None, :] - owner * per_owner
        return (jnp.sum(jnp.where(mine, from_first + 1, 0), axis=-1) - 1).reshape(1, -1)

    parity = slice(0, planes)
    here, there = labels(me, parity), labels(me, slice(planes, owners))
    local = jnp.concatenate([here, there], axis=1)
    parity_local = jnp.concatenate([here, labels(me ^ 1, parity)], axis=0)

    parity_ids, parity_owner, parity_place = near_ids[parity], near_owner[parity], near_place[parity]
    attn_places = jnp.where(parity_owner == me, parity_place, -1)
    attn_places = jnp.where(parity_owner == (me ^ 1), parity_place + capacity, attn_places).reshape(1, -1)
    base = capacity * jnp.arange(planes, dtype=I32)[:, None]
    places = jnp.stack(
        [
            jnp.where(parity_owner == me, parity_place + base, -1),
            jnp.where(parity_owner == (me ^ 1), parity_place + base + planes * capacity, -1),
            parity_ids - me * per_owner,
            parity_ids - (me ^ 1) * per_owner,
        ]
    )
    places = jnp.concatenate([places[:, d : d + 1] for d in order], axis=1).reshape(4, -1)

    first_weight = after(weight, places, local, parity_local, attn_places, slot_order, other_down_t)
    attn_start = after(attn, *first_rows)
    going_down, going_up = attn_line(attn_start, 1, -1), attn_line(attn_start, 1, 1)
    frozen = frozen_part(tensor, (first_weight, other_weight), row_names, plane_rows)
    grad_slots = after(grad_slots, frozen)
    part_grads = token_ranks(slot_order, local, up, grad_slots, per_owner)
    low_grads = sum([flip(part_grads, k) for k in range(1, tensors)], part_grads)
    grad_low = (ADAPTER_SCALE * low_grads).astype(BF16)
    ranks = (grad_low, swap(grad_low))
    downs = (down_t, other_down_t)

    def with_term(i, types):
        return add_term(frozen, i, half * tokens, places, ranks, downs, per_owner, types)

    pairs = with_term(0, [BF16] * planes)
    below, above = [going_down], [going_up]
    for d in range(2, planes):
        if d == 2:
            going_down, going_up = after((going_down, going_up), *pairs)
        going_down, going_up = attn_line(going_down, d, -1), attn_line(going_up, d, 1)
        below.append(going_down)
        above.append(going_up)
    pairs += with_term(1, [BF16] * (planes - 2) + [F32] * 2)
    sums = {d: pairs[2 * i : 2 * i + 2] for i, d in enumerate(order)}
    going_up, going_down = [None, None], [None, None]
    for d in range(planes - 1, 0, -1):
        for i in range(2):
            up_sum, down_sum = sums[d][i], sums[planes - d][i]
            if going_up[i] is not None:
                up_sum = (up_sum.astype(F32) + going_up[i].astype(F32)).astype(BF16)
                down_sum = (down_sum.astype(F32) + going_down[i].astype(F32)).astype(BF16)
            if i == 0:
                last_sums = (up_sum, down_sum)
            going_up[i], going_down[i] = up_line(up_sum, d), down_line(down_sum, d)
    below[-1], above[-1] = after((below[-1], above[-1]), *last_sums)
    attn_own, attn_other, parity_inputs = repack(
        plane, attn_places, parity_local, downs, attn, below, above, capacity, per_owner
    )
    attn_slots = [attn_own, swap(attn_other)]
    low_inputs = sum([flip(parity_inputs, k) for k in range(1, tensors)], parity_inputs)
    up_scaled = (ADAPTER_SCALE * low_inputs).astype(BF16)
    up_scaled = jnp.concatenate([up_scaled[0], swap(up_scaled[1])], axis=1)
    down_grad, up_grad = adapter_gradients(slot_order, local, grad_low, up_scaled, attn_slots, grad_slots, per_owner)
    going_up, going_down = after((going_up, going_down), down_grad)
    total = [x + up_sum.astype(F32) + down_sum.astype(F32) for x, up_sum, down_sum in zip(sums[0], going_up, going_down)]
    attention_output_gradient = jnp.concatenate(total, axis=0).astype(BF16)
    return attention_output_gradient, down_grad, up_grad


def solution(mesh):
    placed = (
        P("adapter", "tensor"),
        P(("adapter", "tensor"), None),
        P("adapter"),
        P("tensor", "adapter"),
        P("tensor", "adapter"),
        P("adapter", "tensor"),
    )
    return jax.shard_map(
        per_device,
        mesh=mesh,
        in_specs=placed,
        out_specs=(P("adapter", "tensor"), P("tensor", "adapter"), P("adapter", "tensor")),
        check_vma=False,
    )
```

```python
import functools

import jax
import jax.numpy as jnp
from jax import lax
from jax.experimental import pallas as pl
from jax.experimental.pallas import tpu as pltpu
from jax.sharding import PartitionSpec as P

ADAPTER_RANK = 16
ADAPTER_SCALE = 2.0
ROWS = 16
F32 = jnp.float32
BF16 = jnp.bfloat16
I32 = jnp.int32
NT = (((1,), (1,)), ((), ()))
VMEM_BYTES = 56 * 1024 * 1024
IN_VMEM = pl.BlockSpec(memory_space=pltpu.VMEM)
IN_SMEM = pl.BlockSpec(memory_space=pltpu.SMEM)
ANYWHERE = pl.BlockSpec(memory_space=pl.ANY)


def cost(flops, nbytes):
    return pl.CostEstimate(flops=int(flops) // 64, bytes_accessed=int(nbytes) // 64, transcendentals=0)


def params():
    return pltpu.CompilerParams(vmem_limit_bytes=VMEM_BYTES)


def pack_kernel(slot_ref, *refs):
    pieces, out_ref = refs[:-1], refs[-1]
    shape = (out_ref.shape[0], slot_ref.shape[1])
    pick = (lax.broadcasted_iota(I32, shape, 0) == slot_ref[...]).astype(F32).astype(BF16)
    rows = jnp.concatenate([piece[...] for piece in pieces], axis=0)
    out_ref[...] = jnp.dot(pick, rows, preferred_element_type=F32).astype(BF16)


def pack_rows(slot, pieces, slots):
    tokens, width = slot.shape[1], pieces[0].shape[1]
    tile = min(1024, width)
    column = lambda n: (0, n)
    return pl.pallas_call(
        pack_kernel,
        grid=(width // tile,),
        out_shape=jax.ShapeDtypeStruct((slots, width), BF16),
        in_specs=[pl.BlockSpec((1, tokens), lambda n: (0, 0))]
        + [pl.BlockSpec((piece.shape[0], tile), column) for piece in pieces],
        out_specs=pl.BlockSpec((slots, tile), column),
        compiler_params=params(),
        cost_estimate=cost(2 * tokens * slots * width, 2 * (tokens + slots) * width),
        name="pack_rows",
    )(slot, *pieces)


def masked_sum(projected, local, per_owner):
    total = jnp.zeros((ADAPTER_RANK, projected.shape[1]), F32)
    for j in range(per_owner):
        total = total + jnp.where(local == j, projected[j * ADAPTER_RANK : (j + 1) * ADAPTER_RANK], 0.0)
    return total


def repack_kernel(planes, per_owner, plane_ref, places_ref, local_ref, own_d_ref, other_d_ref, *refs):
    pieces = refs[: 2 * planes - 1]
    own_ref, other_ref, ranks_ref, rows, downs, sems, down_sems = refs[2 * planes - 1 :]
    here, below, above = pieces[0], pieces[1:planes], pieces[planes:]
    plane = plane_ref[0]

    def copy(source, d):
        return pltpu.make_async_copy(source, rows.at[d], sems.at[d])

    copy(here, 0).start()
    for d in range(1, planes):
        @pl.when(plane + d < planes)
        def _():
            copy(below[d - 1], d).start()

        @pl.when(plane + d >= planes)
        def _():
            copy(above[planes - d - 1], d).start()

    weights = [
        pltpu.make_async_copy(source, downs.at[i], down_sems.at[i]) for i, source in enumerate((own_d_ref, other_d_ref))
    ]
    for weight in weights:
        weight.start()
    tokens = here.shape[0]
    capacity = own_ref.shape[0] // planes
    row = lax.broadcasted_iota(I32, (2 * capacity, tokens), 0)
    for d in range(planes):
        copy(here, d).wait()
        pick = (row == places_ref[:, d * tokens : (d + 1) * tokens]).astype(F32).astype(BF16)
        packed = jnp.dot(pick, rows[d], preferred_element_type=F32).astype(BF16)
        own_ref[pl.ds(d * capacity, capacity), :] = packed[:capacity]
        other_ref[pl.ds(d * capacity, capacity), :] = packed[capacity:]
    for i, out_ref in enumerate((own_ref, other_ref)):
        weights[i].wait()
        projected = lax.dot_general(downs[i], out_ref[...], NT, preferred_element_type=F32)
        ranks_ref[i] = masked_sum(projected, local_ref[i : i + 1, :], per_owner)


def repack(plane, places, local, down_ts, here, below, above, capacity, per_owner):
    tokens, width = here.shape
    planes = len(below) + 1
    slots = planes * capacity
    rank_cols = down_ts[0].shape[0]
    return pl.pallas_call(
        functools.partial(repack_kernel, planes, per_owner),
        out_shape=[jax.ShapeDtypeStruct((slots, width), BF16)] * 2
        + [jax.ShapeDtypeStruct((2, ADAPTER_RANK, slots), F32)],
        in_specs=[IN_SMEM, IN_VMEM, IN_VMEM] + [ANYWHERE] * (2 * planes + 1),
        out_specs=[IN_VMEM] * 3,
        scratch_shapes=[
            pltpu.VMEM((planes, tokens, width), BF16),
            pltpu.VMEM((2, rank_cols, width), BF16),
            pltpu.SemaphoreType.DMA((planes,)),
            pltpu.SemaphoreType.DMA((2,)),
        ],
        compiler_params=params(),
        cost_estimate=cost(4 * slots * (tokens + rank_cols) * width, 2 * planes * (tokens + 2 * capacity) * width),
        name="repack",
    )(plane.reshape(1), places, local, *down_ts, here, *below, *above)


def ranks_kernel(per_owner, blocks, order_ref, local_ref, weight_ref, *refs):
    pieces, (out_ref, projected) = refs[:blocks], refs[blocks:]
    k = pl.program_id(0)
    rows = jnp.concatenate([piece[...] for piece in pieces], axis=0)
    part = lax.dot_general(weight_ref[...], rows, NT, preferred_element_type=F32)

    @pl.when(k == 0)
    def _():
        projected[...] = part

    @pl.when(k > 0)
    def _():
        projected[...] += part

    @pl.when(k == pl.num_programs(0) - 1)
    def _():
        out_ref[...] = masked_sum(projected, local_ref[...], per_owner)


def block_specs(blocks, capacity, tile):
    return [pl.BlockSpec((capacity, tile), lambda n, order, i=i: (order[i], n)) for i in range(blocks)]


def token_ranks(order, local, weight, slots, per_owner):
    blocks, width = order.shape[0], weight.shape[1]
    total = local.shape[1]
    rank_cols = weight.shape[0]
    tile = min(1024, width)
    return pl.pallas_call(
        functools.partial(ranks_kernel, per_owner, blocks),
        out_shape=jax.ShapeDtypeStruct((ADAPTER_RANK, total), F32),
        grid_spec=pltpu.PrefetchScalarGridSpec(
            num_scalar_prefetch=1,
            grid=(width // tile,),
            in_specs=[
                pl.BlockSpec((1, total), lambda n, order: (0, 0)),
                pl.BlockSpec((rank_cols, tile), lambda n, order: (0, n)),
            ]
            + block_specs(blocks, total // blocks, tile),
            out_specs=pl.BlockSpec((ADAPTER_RANK, total), lambda n, order: (0, 0)),
            scratch_shapes=[pltpu.VMEM((rank_cols, total), F32)],
        ),
        compiler_params=params(),
        cost_estimate=cost(2 * total * width * rank_cols, 2 * width * (total + rank_cols)),
        name="token_ranks",
    )(order, local, weight, *[slots] * blocks)


def load_rows(names, place_ref, pieces, rows, sems):
    me = place_ref[0]
    copies = []
    for (first, ks), piece in zip(names, pieces):
        blocks = pl.ds(first, piece.shape[1])
        for j, k in enumerate(ks):
            copies.append(pltpu.make_async_copy(piece.at[j], rows.at[blocks, me ^ k], sems.at[len(copies)]))
            copies[-1].start()
    for copy in copies:
        copy.wait()


def frozen_kernel(names, place_ref, own_w_ref, other_w_ref, *refs):
    pieces, (out_ref, rows, sems) = refs[:-3], refs[-3:]
    blocks, tensors, sub, _ = rows.shape
    tokens = tensors * sub
    depth = own_w_ref.shape[1]

    @pl.when(pl.program_id(0) == 0)
    def _():
        load_rows(names, place_ref, pieces, rows, sems)

    for b in range(blocks):
        x = rows[b].reshape(tokens, 2 * depth)
        product = lax.dot_general(x[:, :depth], own_w_ref[...], NT, preferred_element_type=F32)
        product += lax.dot_general(x[:, depth:], other_w_ref[...], NT, preferred_element_type=F32)
        out_ref[pl.ds(b * tokens, tokens), :] = product


def frozen_part(tensor, weights, names, pieces):
    _, blocks, sub, cols = pieces[0].shape
    blocks, tensors = 2 * blocks, sum(len(ks) for _, ks in names) // 2
    rows = blocks * sub * tensors
    width, depth = weights[0].shape
    tile = min(1024, width)
    return pl.pallas_call(
        functools.partial(frozen_kernel, names),
        grid=(width // tile,),
        out_shape=jax.ShapeDtypeStruct((rows, width), F32),
        in_specs=[IN_SMEM] + [pl.BlockSpec((tile, depth), lambda n: (n, 0))] * 2 + [ANYWHERE] * len(pieces),
        out_specs=pl.BlockSpec((rows, tile), lambda n: (0, n)),
        scratch_shapes=[pltpu.VMEM((blocks, tensors, sub, cols), BF16), pltpu.SemaphoreType.DMA((2 * tensors,))],
        compiler_params=params(),
        cost_estimate=cost(2 * rows * width * cols, 4 * rows * width + 4 * width * depth),
        name="frozen_part",
    )(tensor.reshape(1), *weights, *pieces)


def spread_rows(wide, first, local, ranks, per_owner):
    for j in range(per_owner):
        wide[pl.ds(first + j * ADAPTER_RANK, ADAPTER_RANK), :] = jnp.where(local == j, ranks, 0.0).astype(BF16)


def term_kernel(per_owner, frozen_ref, places_ref, *refs):
    ranks, downs, out_refs, (wide, flat) = refs[:2], refs[2:4], refs[4:-2], refs[-2:]
    rank_cols = downs[0].shape[0]

    @pl.when(pl.program_id(0) == 0)
    def _():
        for i in range(2):
            slot, local = places_ref[i : i + 1, :], places_ref[i + 2 : i + 3, :]
            pick = lax.broadcasted_iota(I32, (ranks[i].shape[1], slot.shape[1]), 0) == slot
            in_order = jnp.dot(ranks[i][...], pick.astype(F32).astype(BF16), preferred_element_type=F32)
            spread_rows(wide, i * rank_cols, local, in_order, per_owner)
        flat[...] = wide[...].T

    total = frozen_ref[...]
    total += jnp.dot(flat[:, :rank_cols], downs[0][...], preferred_element_type=F32)
    total += jnp.dot(flat[:, rank_cols:], downs[1][...], preferred_element_type=F32)
    rows = total.shape[0] // len(out_refs)
    for i, out_ref in enumerate(out_refs):
        out_ref[...] = total[i * rows : (i + 1) * rows].astype(out_ref.dtype)


def add_term(frozen, first, rows, places, ranks, downs, per_owner, types):
    width = frozen.shape[1]
    rank_cols = downs[0].shape[0]
    tile = min(1024, width)
    column = lambda n: (0, n)
    each = rows // len(types)
    return pl.pallas_call(
        functools.partial(term_kernel, per_owner),
        grid=(width // tile,),
        out_shape=[jax.ShapeDtypeStruct((each, width), kind) for kind in types],
        in_specs=[
            pl.BlockSpec((rows, tile), lambda n: (first, n)),
            pl.BlockSpec((places.shape[0], rows), lambda n: (0, first)),
        ]
        + [pl.BlockSpec(x.shape, lambda n: (0, 0)) for x in ranks]
        + [pl.BlockSpec((rank_cols, tile), column)] * 2,
        out_specs=[pl.BlockSpec((each, tile), column)] * len(types),
        scratch_shapes=[pltpu.VMEM((2 * rank_cols, rows), BF16), pltpu.VMEM((rows, 2 * rank_cols), BF16)],
        compiler_params=params(),
        cost_estimate=cost(4 * rows * width * rank_cols, 6 * rows * width + 4 * rank_cols * width),
        name="add_term",
    )(frozen, places, *ranks, *downs)


def gradients_kernel(per_owner, blocks, order_ref, local_ref, grad_ranks_ref, up_ranks_ref, own_ref, other_ref, *refs):
    grad, (down_ref, up_ref, flat_grad, wide_up) = refs[:blocks], refs[blocks:]

    @pl.when(pl.program_id(0) == 0)
    def _():
        local = local_ref[...]
        spread_rows(wide_up, 0, local, grad_ranks_ref[...].astype(F32), per_owner)
        flat_grad[...] = wide_up[...].T
        spread_rows(wide_up, 0, local, up_ranks_ref[...].astype(F32), per_owner)

    rows = jnp.concatenate([own_ref[...], other_ref[...]], axis=0)
    down_ref[...] = lax.dot_general(rows, flat_grad[...], (((0,), (0,)), ((), ())), preferred_element_type=F32)
    rows = jnp.concatenate([piece[...] for piece in grad], axis=0)
    up_ref[...] = jnp.dot(wide_up[...], rows, preferred_element_type=F32)


def adapter_gradients(order, local, grad_ranks, up_ranks, attn, grad, per_owner):
    total, width = grad.shape
    blocks = order.shape[0]
    rank_cols = per_owner * ADAPTER_RANK
    tile = min(512, width)
    whole = lambda n, order: (0, 0)
    column = lambda n, order: (0, n)
    return pl.pallas_call(
        functools.partial(gradients_kernel, per_owner, blocks),
        out_shape=(
            jax.ShapeDtypeStruct((width, rank_cols), F32),
            jax.ShapeDtypeStruct((rank_cols, width), F32),
        ),
        grid_spec=pltpu.PrefetchScalarGridSpec(
            num_scalar_prefetch=1,
            grid=(width // tile,),
            in_specs=[pl.BlockSpec((1, total), whole)]
            + [pl.BlockSpec((ADAPTER_RANK, total), whole)] * 2
            + [pl.BlockSpec((total // 2, tile), column)] * 2
            + block_specs(blocks, total // blocks, tile),
            out_specs=(
                pl.BlockSpec((tile, rank_cols), lambda n, order: (n, 0)),
                pl.BlockSpec((rank_cols, tile), column),
            ),
            scratch_shapes=[pltpu.VMEM((total, rank_cols), BF16), pltpu.VMEM((rank_cols, total), BF16)],
        ),
        compiler_params=params(),
        cost_estimate=cost(4 * total * width * rank_cols, 4 * total * width + 8 * rank_cols * width),
        name="adapter_gradients",
    )(order, local, grad_ranks, up_ranks, *attn, *[grad] * blocks)


def per_device(attn, grad, ids, weight, down, up):
    owners = lax.axis_size("adapter")
    tensors = lax.axis_size("tensor")
    planes = owners // 2
    me = lax.axis_index("adapter")
    plane, core = me // 2, me % 2
    tensor = lax.axis_index("tensor")
    tokens, width = attn.shape
    sub = grad.shape[0]
    out_cols = weight.shape[1]
    rank_cols = down.shape[1]
    per_owner = rank_cols // ADAPTER_RANK
    capacity = -(-5 * tokens // (2 * owners) // ROWS) * ROWS
    slot_count = owners * capacity

    def shift(x, by):
        pairs = [(2 * z + c, 2 * ((z + by) % planes) + c) for z in range(planes) for c in range(2)]
        return lax.ppermute(x, "adapter", pairs)

    def up_line(x, distance):
        pairs = [(2 * z + c, 2 * z + 2 + c) for z in range(planes - distance) for c in range(2)]
        return lax.ppermute(x, "adapter", pairs)

    def down_line(x, distance):
        pairs = [(2 * z + c, 2 * z - 2 + c) for z in range(distance, planes) for c in range(2)]
        return lax.ppermute(x, "adapter", pairs)

    def attn_line(x, d, way):
        planes_on = range(d - 1, planes - 1) if way == 1 else range(1, planes - d + 1)
        return lax.ppermute(x, "adapter", [(2 * z + c, 2 * (z + way) + c) for z in planes_on for c in range(2)])

    def swap(x):
        return lax.ppermute(x, "adapter", [(a, a ^ 1) for a in range(owners)])

    def flip(x, k):
        return lax.ppermute(x, "tensor", [(t, t ^ k) for t in range(tensors)])

    def after(x, *others):
        return lax.optimization_barrier((x, *others))[0]

    def tensor_cols(k):
        return lax.dynamic_slice_in_dim(grad, (tensor ^ k) * width, width, 1)

    tensor_parts = [tensor_cols(k) for k in range(tensors)]
    grad_rows = tensor_parts[:1] + [flip(tensor_parts[k], k) for k in range(1, tensors)]
    grad_again, ids_again = after((grad, ids), *tensor_parts)

    def plane_cols(offset):
        p = (plane + offset) % planes
        parts = [
            lax.dynamic_slice_in_dim(grad_again, (2 * p + c) * out_cols, out_cols, 1) for c in (core, 1 - core)
        ]
        return jnp.concatenate(parts, axis=1)

    half = planes // 2
    order = [d for s in range(1, half) for d in (s, planes - s)] + [half, 0]
    plane_parts = [plane_cols(d) for d in range(planes)]
    part = {0: plane_parts[0]}
    for d in range(1, planes):
        part[planes - d] = shift(plane_parts[d], d)
    ids_again = after(ids_again, *plane_parts, *grad_rows[1:])

    all_ids = lax.all_to_all(jnp.broadcast_to(ids_again, (owners, tokens)), "adapter", 0, 0, tiled=True)

    def placing(block_ids):
        owner = block_ids // per_owner
        earlier = jnp.arange(tokens)[:, None] > jnp.arange(tokens)[None, :]
        same = owner[..., :, None] == owner[..., None, :]
        place = jnp.sum((same & earlier).astype(I32), axis=-1)
        return owner, place

    owner, place = placing(ids)
    slot = owner * capacity + place
    slot_here = jnp.concatenate(
        [lax.dynamic_slice_in_dim(slot, (tensor ^ k) * sub, sub, 0) for k in range(tensors)]
    )
    down_t = down.T
    grad_packed = pack_rows(slot_here.reshape(1, -1), after(grad_rows, down_t), slot_count)

    def to_owners(x):
        x = x.reshape(owners, capacity, width)
        return lax.all_to_all(x, "adapter", 0, 0, tiled=True).reshape(slot_count, width)

    grad_packed = after(grad_packed, part[1], part[planes - 1])
    grad_slots = to_owners(grad_packed)

    halves = [jnp.stack([part[d] for d in order[i * half : (i + 1) * half]], axis=0) for i in range(2)]
    bits = [1 << i for i in range(tensors.bit_length() - 1)]
    plane_rows = [[([0], x[None])] for x in halves]
    for step in zip(bits, reversed(bits)):
        for rows, bit in zip(plane_rows, step):
            sent = jnp.concatenate([x for _, x in rows], axis=0) if len(rows) > 1 else rows[0][1]
            rows.append(([k ^ bit for ks, _ in rows for k in ks], flip(sent, bit)))
    first_rows = [rows[1][1] for rows in plane_rows]
    row_names = [(i * half, ks) for i, rows in enumerate(plane_rows) for ks, _ in rows]
    plane_rows = [x for rows in plane_rows for _, x in rows]
    all_ids = after(all_ids, *first_rows)
    other_weight = swap(weight)
    other_down_t = swap(down_t)

    ahead = [2 * ((plane + jnp.arange(planes)) % planes) + c for c in (core, 1 - core)]
    slot_order = jnp.concatenate(ahead)
    near_ids = all_ids[slot_order]
    near_owner, near_place = placing(near_ids)

    def labels(owner, blocks):
        mine = (near_owner[blocks] == owner)[:, None, :]
        mine &= near_place[blocks][:, None, :] == jnp.arange(capacity, dtype=I32)[:, None]
        from_first = near_ids[blocks][:, None, :] - owner * per_owner
        return (jnp.sum(jnp.where(mine, from_first + 1, 0), axis=-1) - 1).reshape(1, -1)

    parity = slice(0, planes)
    here, there = labels(me, parity), labels(me, slice(planes, owners))
    local = jnp.concatenate([here, there], axis=1)
    parity_local = jnp.concatenate([here, labels(me ^ 1, parity)], axis=0)

    parity_ids, parity_owner, parity_place = near_ids[parity], near_owner[parity], near_place[parity]
    attn_places = jnp.where(parity_owner == me, parity_place, -1)
    attn_places = jnp.where(parity_owner == (me ^ 1), parity_place + capacity, attn_places).reshape(1, -1)
    base = capacity * jnp.arange(planes, dtype=I32)[:, None]
    places = jnp.stack(
        [
            jnp.where(parity_owner == me, parity_place + base, -1),
            jnp.where(parity_owner == (me ^ 1), parity_place + base + planes * capacity, -1),
            parity_ids - me * per_owner,
            parity_ids - (me ^ 1) * per_owner,
        ]
    )
    places = jnp.concatenate([places[:, d : d + 1] for d in order], axis=1).reshape(4, -1)

    first_weight = after(weight, places, local, parity_local, attn_places, slot_order, other_down_t)
    attn_start = after(attn, *first_rows)
    going_down, going_up = attn_line(attn_start, 1, -1), attn_line(attn_start, 1, 1)
    frozen = frozen_part(tensor, (first_weight, other_weight), row_names, plane_rows)
    grad_slots = after(grad_slots, frozen)
    part_grads = token_ranks(slot_order, local, up, grad_slots, per_owner)
    low_grads = sum([flip(part_grads, k) for k in range(1, tensors)], part_grads)
    grad_low = (ADAPTER_SCALE * low_grads).astype(BF16)
    ranks = (grad_low, swap(grad_low))
    downs = (down_t, other_down_t)

    def with_term(i, types):
        return add_term(frozen, i, half * tokens, places, ranks, downs, per_owner, types)

    pairs = with_term(0, [BF16] * planes)
    below, above = [going_down], [going_up]
    for d in range(2, planes):
        if d == 2:
            going_down, going_up = after((going_down, going_up), *pairs)
        going_down, going_up = attn_line(going_down, d, -1), attn_line(going_up, d, 1)
        below.append(going_down)
        above.append(going_up)
    pairs += with_term(1, [BF16] * (planes - 2) + [F32] * 2)
    sums = {d: pairs[2 * i : 2 * i + 2] for i, d in enumerate(order)}
    going_up, going_down = [None, None], [None, None]
    for d in range(planes - 1, 0, -1):
        for i in range(2):
            up_sum, down_sum = sums[d][i], sums[planes - d][i]
            if going_up[i] is not None:
                up_sum = (up_sum.astype(F32) + going_up[i].astype(F32)).astype(BF16)
                down_sum = (down_sum.astype(F32) + going_down[i].astype(F32)).astype(BF16)
            if i == 0:
                last_sums = (up_sum, down_sum)
            going_up[i], going_down[i] = up_line(up_sum, d), down_line(down_sum, d)
    below[-1], above[-1] = after((below[-1], above[-1]), *last_sums)
    attn_own, attn_other, parity_inputs = repack(
        plane, attn_places, parity_local, downs, attn, below, above, capacity, per_owner
    )
    attn_slots = [attn_own, swap(attn_other)]
    low_inputs = sum([flip(parity_inputs, k) for k in range(1, tensors)], parity_inputs)
    up_scaled = (ADAPTER_SCALE * low_inputs).astype(BF16)
    up_scaled = jnp.concatenate([up_scaled[0], swap(up_scaled[1])], axis=1)
    down_grad, up_grad = adapter_gradients(slot_order, local, grad_low, up_scaled, attn_slots, grad_slots, per_owner)
    going_up, going_down = after((going_up, going_down), down_grad)
    total = [x + up_sum.astype(F32) + down_sum.astype(F32) for x, up_sum, down_sum in zip(sums[0], going_up, going_down)]
    attention_output_gradient = jnp.concatenate(total, axis=0).astype(BF16)
    return attention_output_gradient, down_grad, up_grad


def solution(mesh):
    placed = (
        P("adapter", "tensor"),
        P(("adapter", "tensor"), None),
        P("adapter"),
        P("tensor", "adapter"),
        P("tensor", "adapter"),
        P("adapter", "tensor"),
    )
    return jax.shard_map(
        per_device,
        mesh=mesh,
        in_specs=placed,
        out_specs=(P("adapter", "tensor"), P("tensor", "adapter"), P("adapter", "tensor")),
        check_vma=False,
    )
```
